32 devices in a mesh: space: 4 (over z), chan: 8 (over y, x, core).
Axes of the slice: x: 2, y: 2, z: 4, core: 2. Of those that a mesh axis runs over, the one named last changes fastest.
Arguments:
- images: bfloat16 [512, 16, 16, 128], P('chan', None, 'space'), may hold values from -6 to 6
- depth_filter: float32 [27, 512], P(None, 'chan'), may hold values from -1.25 to 1.25
- point_filter: bfloat16 [512, 512], P('chan'), may hold values from -0.25 to 0.25
- grad_out: bfloat16 [512, 16, 16, 128], P('chan', None, 'space'), may hold values from -6 to 6
Outputs:
- block_out: bfloat16 [512, 16, 16, 128], P('chan', None, 'space')
- point_grad: float32 [512, 512], P('chan', 'space')
- input_grad: bfloat16 [512, 16, 16, 128], P('chan', None, 'space')
- depth_grad: float32 [27, 512], P(None, 'chan')
The draws below stay inside these ranges and needn't reach their ends.
All inputs are finite; a program needn't handle non-finite values.
Results may differ from the reference program's by a relative error of at most 0.0049.
Values may be sent and summed in bfloat16 or wider, within the bound.
No kernel may reach another device: no remote copies, remote signals or barrier semaphores. Data moves between devices by JAX's collectives and lax.ppermute only.
A program may use at most 128 MiB of HBM per device.

```python
import math
import jax
import jax.numpy as jnp
from jax import lax

C = 512
PLANES = 16
WIDTH = 128
ROWS = 16
CELLS = 32768


def steps_of(rng, shape, split, smallest, largest):
    gain = 1.0
    for dim, parts in split:
        heights = jax.random.uniform(jax.random.fold_in(jax.random.fold_in(rng, 6), dim), (parts,), jnp.float32, smallest / len(split), largest / len(split))
        gain = gain * jnp.repeat(jnp.exp(heights), shape[dim] // parts).reshape((-1,) + (1,) * (len(shape) - 1 - dim))
    return gain


def normal_values(rng, shape, scale, most, cuts=(), held_as=jnp.bfloat16):
    level = steps_of(rng, shape, cuts, -0.22, 0.18) if cuts else 1.0
    drawn = jax.random.normal(rng, shape, jnp.float32) * scale * level
    return jnp.minimum(jnp.maximum(drawn, -most), most).astype(held_as)


def setup_inputs(seed: int = 0) -> dict:
    key_list = jax.random.split(jax.random.key(seed), 5)
    return {
        "images": normal_values(key_list[0], (C, PLANES, ROWS, WIDTH), 1.0, 6.0, ((0, 8), (2, 4))),
        "depth_filter": normal_values(key_list[1], (27, C), 27 ** -0.5, 1.25, ((1, 8),), jnp.float32),
        "point_filter": normal_values(key_list[2], (C, C), C ** -0.5, 0.25, ((0, 8),)),
        "grad_out": normal_values(key_list[3], (C, PLANES, ROWS, WIDTH), 1.0, 6.0, ((0, 8), (2, 4))),
    }


def depth_forward(padded, tap_weights, planes, row_count, col_count):
    summed = jnp.zeros((padded.shape[0], planes, row_count, col_count), jnp.float32)
    for tap_index in range(27):
        plane_off, row_off, col_off = (tap_index // 9, tap_index // 3 % 3, tap_index % 3)
        window = padded[:, plane_off:plane_off + planes, row_off:row_off + row_count, col_off:col_off + col_count]
        summed = summed + tap_weights[tap_index][:, None, None, None] * window.astype(jnp.float32)
    return summed

def depth_backward(padded, tap_weights, planes, row_count, col_count):
    summed = jnp.zeros((padded.shape[0], planes, row_count, col_count), jnp.float32)
    for tap_index in range(27):
        plane_off, row_off, col_off = (2 - tap_index // 9, 2 - tap_index // 3 % 3, 2 - tap_index % 3)
        window = padded[:, plane_off:plane_off + planes, row_off:row_off + row_count, col_off:col_off + col_count]
        summed = summed + tap_weights[tap_index][:, None, None, None] * window.astype(jnp.float32)
    return summed

def tap_sums(padded, back_hidden, planes, row_count, col_count):
    collected = []
    for tap_index in range(27):
        plane_off, row_off, col_off = (tap_index // 9, tap_index // 3 % 3, tap_index % 3)
        window = padded[:, plane_off:plane_off + planes, row_off:row_off + row_count, col_off:col_off + col_count]
        collected.append(lax.optimization_barrier(jnp.sum(window.astype(jnp.float32) * back_hidden.astype(jnp.float32), axis=(1, 2, 3))))
    return jnp.stack(collected)

def reference(images, depth_filter, point_filter, grad_out):
    chan_count, planes, row_count, col_count = images.shape
    grad_scale = 1.0 / math.sqrt(CELLS)
    padding = ((0, 0), (1, 1), (1, 1), (1, 1))
    padded_in = jnp.pad(images, padding)
    hidden = depth_forward(padded_in, depth_filter, planes, row_count, col_count).astype(jnp.bfloat16)
    flat_hidden = hidden.reshape(chan_count, -1)
    flat_grad = grad_out.reshape(chan_count, -1)
    block_out = jnp.dot(point_filter, flat_hidden, preferred_element_type=jnp.float32).astype(jnp.bfloat16).reshape(images.shape)
    point_grad = lax.dot_general(flat_grad, flat_hidden, (((1,), (1,)), ((), ())), preferred_element_type=jnp.float32) * grad_scale
    back_hidden = lax.dot_general(point_filter, flat_grad, (((0,), (0,)), ((), ())), preferred_element_type=jnp.float32)
    back_hidden = back_hidden.astype(jnp.bfloat16).reshape(images.shape)
    padded_back = jnp.pad(back_hidden, padding)
    input_grad = depth_backward(padded_back, depth_filter, planes, row_count, col_count).astype(jnp.bfloat16)
    depth_grad = tap_sums(padded_in, back_hidden, planes, row_count, col_count) * grad_scale
    return (block_out, point_grad, input_grad, depth_grad)
```

```python
import math

import jax
import jax.numpy as jnp
from jax import lax
from jax.experimental import pallas as pl
from jax.experimental.pallas import tpu as pltpu
from jax.sharding import PartitionSpec as P

F32, BF16 = jnp.float32, jnp.bfloat16
IN_VMEM = pl.BlockSpec(memory_space=pltpu.VMEM)


class Place:
    def __init__(self, count):
        self.mids = 2
        self.his = count // 4
        index = lax.axis_index("chan")
        self.core = index % 2
        self.mid = index // 2 % self.mids
        self.hi = index // 2 // self.mids

    def block(self, hi_back, mid_back, core_flip):
        hi = (self.hi + self.his - hi_back) % self.his
        mid = (self.mid + self.mids - mid_back) % self.mids
        core = 1 - self.core if core_flip else self.core
        return hi, mid, core

    def flat(self, hi, mid, core):
        return (hi * self.mids + mid) * 2 + core


def kernel_call(kernel, outs, args, scratch=(), micros=2.0):
    moved = sum(a.size * a.dtype.itemsize for a in args) + sum(math.prod(o.shape) * o.dtype.itemsize for o in outs)
    return pl.pallas_call(
        kernel,
        out_shape=outs,
        in_specs=[IN_VMEM] * len(args),
        out_specs=[IN_VMEM] * len(outs),
        scratch_shapes=list(scratch),
        compiler_params=pltpu.CompilerParams(vmem_limit_bytes=40 * 2**20),
        cost_estimate=pl.CostEstimate(flops=int(micros * 1e9), bytes_accessed=moved, transcendentals=0),
    )(*args)


def shaped(shape, dtype=BF16):
    return jax.ShapeDtypeStruct(shape, dtype)


def raw_to_cells(raw, flat):
    chans, planes, rows, _ = raw.shape

    @pl.loop(0, chans)
    def _(c):
        for p in range(planes):
            flat[pl.ds(p * rows * chans + c, rows, stride=chans), :] = raw[c, p].astype(F32)


def cells_to_raw(flat, raw):
    chans, planes, rows, _ = raw.shape

    @pl.loop(0, chans)
    def _(c):
        for p in range(planes):
            raw[c, p] = flat[pl.ds(p * rows * chans + c, rows, stride=chans), :].astype(raw.dtype)


def relayout_images(images):
    chans, planes, rows, width = images.shape

    def kernel(raw, cells, top, bottom, flat):
        raw_to_cells(raw, flat)

        @pl.loop(0, planes)
        def _(p):
            for r in range(rows):
                value = flat[pl.ds(pl.multiple_of((p * rows + r) * chans, chans), chans), :].astype(BF16)
                cells[p * rows + r] = value
                if r == 0:
                    top[p] = value
                if r == rows - 1:
                    bottom[p] = value

    edge = shaped((planes, chans, width))
    return kernel_call(
        kernel,
        [shaped((planes * rows, chans, width)), edge, edge],
        [images],
        [pltpu.VMEM((planes * rows * chans, width), F32)],
        1.5,
    )


def relayout_grad(grad_out, count):
    chans, planes, rows, width = grad_out.shape
    half = planes * rows // 2

    def kernel(raw, own, other, flat):
        core = Place(count).core
        raw_to_cells(raw, flat)

        @pl.loop(0, half)
        def _(i):
            for out, which in ((own, core), (other, 1 - core)):
                start = pl.multiple_of((which * half + i) * chans, chans)
                out[i] = flat[pl.ds(start, chans), :].astype(BF16)

    part = shaped((half, chans, width))
    return kernel_call(
        kernel, [part, part], [grad_out], [pltpu.VMEM((planes * rows * chans, width), F32)], 1.5
    )


def tap_planes(weights, spread, chans, width):
    turned = jnp.concatenate([weights, jnp.zeros((5, chans), F32)], axis=0).T
    for k in range(27):
        spread[k] = jnp.broadcast_to(turned[:, k : k + 1], (chans, width))


def fill_rims(padded, up, down, planes, rows):
    blank = jnp.zeros(padded.shape[1:], F32)
    for r in range(rows + 2):
        padded[r] = blank
        padded[(planes + 1) * (rows + 2) + r] = blank

    @pl.loop(0, planes)
    def _(p):
        padded[(p + 1) * (rows + 2)] = up(p).astype(F32)
        padded[(p + 1) * (rows + 2) + rows + 1] = down(p).astype(F32)


def depthwise(padded, spread, first, count, rows, store, flipped):
    _, chans, width = padded.shape
    lane = lax.broadcasted_iota(jnp.int32, (16, width), 1)

    @pl.loop(0, count)
    def _(i):
        for start in range(0, chans, 16):
            group = slice(start, start + 16)
            sums = [[None] * 3 for _ in range(rows)]
            for a in range(3):
                for line in range(rows + 2):
                    cells = padded[(first + i + a) * (rows + 2) + line, group]
                    for b in range(3):
                        r = line - b
                        if 0 <= r < rows:
                            for e in range(3):
                                tap = 9 * a + 3 * b + e
                                term = spread[26 - tap if flipped else tap, group] * cells
                                sums[r][e] = term if sums[r][e] is None else sums[r][e] + term
            for r in range(rows):
                before = jnp.where(lane == 0, 0.0, pltpu.roll(sums[r][0], 1, 1))
                after = jnp.where(lane == width - 1, 0.0, pltpu.roll(sums[r][2], width - 1, 1))
                store(i, r, group, sums[r][1] + before + after)


def hidden_halves(cells, up, down, weights, count, planes, rows):
    _, chans, width = cells.shape
    half = planes // 2

    def kernel(cells, up, down, weights, own, other, padded, spread):
        core = Place(count).core
        tap_planes(weights[...], spread, chans, width)
        fill_rims(padded, lambda p: up[p], lambda p: down[p], planes, rows)

        @pl.loop(0, planes)
        def _(p):
            for r in range(rows):
                padded[(p + 1) * (rows + 2) + r + 1] = cells[p * rows + r].astype(F32)

        for out, which in ((own, core), (other, 1 - core)):

            def store(i, r, group, value, out=out):
                out[i * rows + r, group] = value.astype(BF16)

            depthwise(padded, spread, which * half, half, rows, store, False)

    part = shaped((half * rows, chans, width))
    return kernel_call(
        kernel,
        [part, part],
        [cells, up, down, weights],
        [pltpu.VMEM(((planes + 2) * (rows + 2), chans, width), F32), pltpu.VMEM((27, chans, width), F32)],
        5.0,
    )


def picked(table, starts, chans):
    total, wide = table.shape[1], len(starts) * chans
    col = lax.broadcasted_iota(jnp.int32, (total, wide), 1)
    row = lax.broadcasted_iota(jnp.int32, (total, wide), 0)
    want = jnp.zeros((total, wide), jnp.int32)
    for b, start in enumerate(starts):
        want = jnp.where((col >= b * chans) & (col < (b + 1) * chans), start + col - b * chans, want)
    choice = jnp.where(row == want, 1.0, 0.0).astype(BF16)
    return jnp.dot(table, choice, preferred_element_type=F32).astype(BF16)


def pack_grad(own, arrived, filter_own, filter_arrived, count):
    half, chans, width = own.shape
    part = half // 2
    his, mids = count // 4, 2
    hi_slices, mid_slices = mids * 2 * chans // width, his * 2 * chans // width

    def kernel(own, arrived, filter_own, filter_arrived, *outs):
        place = Place(count)
        table = jnp.concatenate([filter_own[...], filter_arrived[...]], axis=0)
        to_hi, to_mid = outs[: his - 1], outs[his - 1 : his + mids - 2]
        mine_hi, mine_mid = outs[-2:]

        def columns(for_hi, hi, mid):
            if for_hi:
                cells = [(hi, (mid + mids - t) % mids) for t in range(mids)]
            else:
                cells = [((hi + his - s) % his, mid) for s in range(his)]
            starts = [
                place.flat(hi_, mid_, place.core if q == 0 else 1 - place.core) * chans
                for hi_, mid_ in cells
                for q in range(2)
            ]
            return picked(table, starts, chans)

        def put(out, base, value):
            for i in range(value.shape[1] // width):
                out[base + i] = value[:, i * width : (i + 1) * width]

        for refs, offset in ((to_hi, 0), (to_mid, part)):

            @pl.loop(0, part)
            def _(i):
                for ref in refs:
                    ref[i, :chans] = own[offset + i]
                    ref[i, chans:] = arrived[offset + i]

        for s, ref in enumerate(to_hi, 1):
            put(ref, part, columns(True, (place.hi + s) % his, place.mid))
        for t, ref in enumerate(to_mid, 1):
            put(ref, part, columns(False, place.hi, (place.mid + t) % mids))
        put(mine_hi, 0, columns(True, place.hi, place.mid))
        put(mine_mid, 0, columns(False, place.hi, place.mid))

    outs = (
        [shaped((part + hi_slices, 2 * chans, width))] * (his - 1)
        + [shaped((part + mid_slices, 2 * chans, width))] * (mids - 1)
        + [shaped((hi_slices, 2 * chans, width)), shaped((mid_slices, 2 * chans, width))]
    )
    outs = kernel_call(kernel, outs, [own, arrived, filter_own, filter_arrived], (), 1.5)
    return outs[: his - 1], outs[his - 1 : his + mids - 2], outs[-2], outs[-1]


def back_terms(mine, arrived, filter_mine, sends):
    slices, both, width = filter_mine.shape
    part = mine.shape[0] - slices
    sources = 1 + len(arrived)
    wide = slices * width
    step = math.gcd(part, 4)

    def kernel(mine, filter_mine, *refs):
        blocks = [mine, *refs[: sources - 1]]
        outs, block_ref = refs[sources - 1 : -1], refs[-1]
        rows = [jnp.concatenate([filter_mine[i] for i in range(slices)], axis=1)]
        for ref in blocks[1:]:
            rows.append(jnp.concatenate([ref[part + i] for i in range(slices)], axis=1))
        block = jnp.concatenate(rows, axis=0)
        block_ref[...] = block
        turned = block.astype(F32).T.astype(BF16)

        @pl.loop(0, part // step)
        def _(i):
            cells = jnp.concatenate(
                [jnp.concatenate([ref[i * step + j] for ref in blocks], axis=0) for j in range(step)], axis=1
            )
            product = jnp.dot(turned, cells, preferred_element_type=F32).astype(BF16)
            for n, out in enumerate(outs):
                for j in range(step):
                    out[i * step + j] = product[n * both : (n + 1) * both, j * width : (j + 1) * width]

    term = shaped((part, both, width))
    outs = kernel_call(
        kernel,
        [term] * (sends + 1) + [shaped((sources * both, wide))],
        [mine, filter_mine, *arrived],
        (),
        2.0,
    )
    return outs[0], outs[1:-1], outs[-1]


def summed_halves(first, second):
    part, both, width = first[0].shape
    chans = both // 2

    def kernel(*refs):
        own, other = refs[-2:]
        for base, terms in ((0, refs[: len(first)]), (part, refs[len(first) : -2])):

            @pl.loop(0, part)
            def _(i):
                total = terms[0][i].astype(F32)
                for term in terms[1:]:
                    total = total + term[i].astype(F32)
                own[base + i] = total[:chans].astype(BF16)
                other[base + i] = total[chans:].astype(BF16)

    out = shaped((2 * part, chans, width))
    return kernel_call(kernel, [out, out], [*first, *second], (), 0.8)


def edge_rows(own, arrived, rows):
    half, chans, width = own.shape
    planes = half // rows

    def kernel(own, arrived, top, bottom):
        @pl.loop(0, planes)
        def _(p):
            for ref, base in ((own, 0), (arrived, planes)):
                top[base + p] = ref[p * rows]
                bottom[base + p] = ref[p * rows + rows - 1]

    edge = shaped((2 * planes, chans, width))
    return kernel_call(kernel, [edge, edge], [own, arrived], (), 0.5)


def joined(own, arrived):
    half, chans, width = own.shape
    part = half // 2

    def kernel(own, arrived, first, second):
        @pl.loop(0, part)
        def _(i):
            for out, base in ((first, 0), (second, part)):
                out[i, :chans] = own[base + i]
                out[i, chans:] = arrived[base + i]

    out = shaped((part, 2 * chans, width))
    return kernel_call(kernel, [out, out], [own, arrived], (), 0.8)


def out_terms(filter_block, hiddens, grads, count, over_mid):
    part, both, width = hiddens[0].shape
    chans = both // 2
    step = math.gcd(part, 4)
    rows_of, cols_of = len(grads), len(hiddens)

    def kernel(block, *refs):
        place = Place(count)
        hidden, grad = refs[:cols_of], refs[cols_of : cols_of + rows_of]
        outs = refs[cols_of + rows_of : cols_of + 2 * rows_of]
        pg_own, pg_other, ordered, lined = refs[cols_of + 2 * rows_of :]
        for j in range(part):
            span = slice(j * width, (j + 1) * width)
            for n, ref in enumerate(hidden):
                hi, mid, _ = place.block(0, n, 0) if over_mid else place.block(n, 0, 0)
                for q in range(2):
                    core = 1 - place.core if q else place.core
                    at = pl.multiple_of(((mid if over_mid else hi) * 2 + core) * chans, chans)
                    ordered[pl.ds(at, chans), span] = ref[j, q * chans : (q + 1) * chans]
            for n, ref in enumerate(grad):
                for q in range(2):
                    lined[q, n * chans : (n + 1) * chans, span] = ref[j, q * chans : (q + 1) * chans]

        weights = block[...]

        @pl.loop(0, part // step)
        def _(i):
            cells = jnp.concatenate(
                [jnp.concatenate([ref[i * step + j] for ref in hidden], axis=0) for j in range(step)], axis=1
            )
            product = jnp.dot(weights, cells, preferred_element_type=F32).astype(BF16)
            for n, out in enumerate(outs):
                for j in range(step):
                    out[i * step + j] = product[n * both : (n + 1) * both, j * width : (j + 1) * width]

        for q, out in enumerate((pg_own, pg_other)):
            out[...] = lax.dot_general(
                lined[q], ordered[...], (((1,), (1,)), ((), ())), preferred_element_type=F32
            )

    term = shaped((part, both, width))
    grad_term = shaped((rows_of * chans, cols_of * both), F32)
    outs = kernel_call(
        kernel,
        [term] * rows_of + [grad_term, grad_term],
        [filter_block, *hiddens, *grads],
        [pltpu.VMEM((cols_of * both, part * width), BF16), pltpu.VMEM((2, rows_of * chans, part * width), BF16)],
        3.0,
    )
    return outs[0], outs[1:rows_of], outs[-2], outs[-1]


def to_raw(own, arrived, count, planes, rows):
    half, chans, width = own.shape

    def kernel(own, arrived, raw, flat):
        core = Place(count).core

        @pl.loop(0, half)
        def _(i):
            for ref, which in ((own, core), (arrived, 1 - core)):
                start = pl.multiple_of((which * half + i) * chans, chans)
                flat[pl.ds(start, chans), :] = ref[i].astype(F32)

        cells_to_raw(flat, raw)

    return kernel_call(
        kernel,
        [shaped((chans, planes, rows, width))],
        [own, arrived],
        [pltpu.VMEM((planes * rows * chans, width), F32)],
        1.5,
    )[0]


def input_gradient(own, arrived, up, down, weights, count, planes, rows):
    half, chans, width = own.shape

    def kernel(own, arrived, up, down, weights, raw, padded, spread, flat):
        core = Place(count).core
        tap_planes(weights[...], spread, chans, width)

        def turned(ref):
            return lambda p: ref[(p + core * (planes // 2)) % planes]

        fill_rims(padded, turned(up), turned(down), planes, rows)

        @pl.loop(0, planes // 2)
        def _(p):
            for ref, which in ((own, core), (arrived, 1 - core)):
                plane = which * (planes // 2) + p
                for r in range(rows):
                    padded[(plane + 1) * (rows + 2) + r + 1] = ref[p * rows + r].astype(F32)

        def store(i, r, group, value):
            start = pl.multiple_of((i * rows + r) * chans + group.start, 16)
            flat[pl.ds(start, 16), :] = value

        depthwise(padded, spread, 0, planes, rows, store, True)
        cells_to_raw(flat, raw)

    return kernel_call(
        kernel,
        [shaped((chans, planes, rows, width))],
        [own, arrived, up, down, weights],
        [
            pltpu.VMEM(((planes + 2) * (rows + 2), chans, width), F32),
            pltpu.VMEM((27, chans, width), F32),
            pltpu.VMEM((planes * rows * chans, width), F32),
        ],
        6.0,
    )[0]


def tap_gradient(cells, up, down, own, arrived, count, planes, rows):
    _, chans, width = cells.shape

    def kernel(cells, up, down, own, arrived, out, padded, back, sums):
        core = Place(count).core
        fill_rims(padded, lambda p: up[p], lambda p: down[p], planes, rows)

        @pl.loop(0, planes)
        def _(p):
            for r in range(rows):
                padded[(p + 1) * (rows + 2) + r + 1] = cells[p * rows + r].astype(F32)

        @pl.loop(0, planes // 2)
        def _(p):
            for ref, which in ((own, core), (arrived, 1 - core)):
                plane = which * (planes // 2) + p
                for r in range(rows):
                    back[plane * rows + r] = ref[p * rows + r].astype(F32)

        lane = lax.broadcasted_iota(jnp.int32, (8, width), 1)

        @pl.loop(0, chans // 8)
        def _(g):
            group = pl.ds(pl.multiple_of(g * 8, 8), 8)

            def step(p, totals):
                totals = list(totals)
                for r in range(rows):
                    here = back[p * rows + r, group]
                    later = jnp.where(lane == width - 1, 0.0, pltpu.roll(here, width - 1, 1))
                    earlier = jnp.where(lane == 0, 0.0, pltpu.roll(here, 1, 1))
                    for a in range(3):
                        for b in range(3):
                            image = padded[(p + a) * (rows + 2) + r + b, group]
                            for e, moved in enumerate((later, here, earlier)):
                                tap = 9 * a + 3 * b + e
                                totals[tap] = totals[tap] + image * moved
                return tuple(totals)

            totals = lax.fori_loop(0, planes, step, tuple(jnp.zeros((8, width), F32) for _ in range(27)))
            for tap in range(27):
                sums[tap, group] = totals[tap]

        out[...] = lax.dot_general(
            jnp.ones((8, width), F32),
            sums[...].reshape(27 * chans, width),
            (((1,), (1,)), ((), ())),
            precision=lax.Precision.HIGHEST,
            preferred_element_type=F32,
        )

    return kernel_call(
        kernel,
        [shaped((8, 27 * chans), F32)],
        [cells, up, down, own, arrived],
        [
            pltpu.VMEM(((planes + 2) * (rows + 2), chans, width), F32),
            pltpu.VMEM((planes * rows, chans, width), F32),
            pltpu.VMEM((27, chans, width), F32),
        ],
        6.0,
    )[0]


def body(images, depth_filter, point_filter, grad_out):
    chans, planes, rows, width = images.shape
    count, slabs = lax.axis_size("chan"), lax.axis_size("space")
    his, mids = count // 4, 2
    place = Place(count)
    grad_scale = 1.0 / math.sqrt(planes * rows * width * slabs)

    def moved(value, target):
        pairs = []
        for i in range(count):
            hi, mid, core = target(i // 2 // mids, i // 2 % mids, i % 2)
            pairs.append((i, (hi % his * mids + mid % mids) * 2 + core))
        return lax.ppermute(value, "chan", pairs)

    def to_core(value):
        return moved(value, lambda hi, mid, core: (hi, mid, 1 - core))

    def along_hi(value, by):
        return moved(value, lambda hi, mid, core: (hi + by, mid, core))

    def along_mid(value, by):
        return moved(value, lambda hi, mid, core: (hi, mid + by, core))

    def halo(top, bottom):
        up = lax.ppermute(bottom, "space", [(i, i + 1) for i in range(slabs - 1)])
        down = lax.ppermute(top, "space", [(i + 1, i) for i in range(slabs - 1)])
        return up, down

    filter_arrived = to_core(point_filter)
    grad_own, grad_other = relayout_grad(grad_out, count)
    grad_arrived = to_core(grad_other)
    to_hi, to_mid, filter_hi, filter_mid = pack_grad(grad_own, grad_arrived, point_filter, filter_arrived, count)
    grads_hi = [along_hi(value, s) for s, value in enumerate(to_hi, 1)]
    grads_mid = [along_mid(value, t) for t, value in enumerate(to_mid, 1)]

    cells, top, bottom = relayout_images(images)
    image_up, image_down = halo(top, bottom)
    hidden_own, hidden_other = hidden_halves(cells, image_up, image_down, depth_filter, count, planes, rows)
    hidden_first, hidden_second = joined(hidden_own, to_core(hidden_other))
    hiddens_mid = [hidden_first] + [along_mid(hidden_first, t) for t in range(1, mids)]
    hiddens_hi = [hidden_second] + [along_hi(hidden_second, s) for s in range(1, his)]

    keep_first, send_first, block_first = back_terms(to_hi[0], grads_hi, filter_hi, mids - 1)
    keep_second, send_second, block_second = back_terms(to_mid[0], grads_mid, filter_mid, his - 1)
    back_first = [keep_first] + [along_mid(value, -t) for t, value in enumerate(send_first, 1)]
    back_second = [keep_second] + [along_hi(value, -s) for s, value in enumerate(send_second, 1)]
    back_own, back_other = summed_halves(back_first, back_second)
    back_arrived = to_core(back_other)
    back_up, back_down = halo(*edge_rows(back_own, back_arrived, rows))

    keep_first, send_first, pg_first, pg_first_other = out_terms(
        block_first, hiddens_mid, [to_hi[0], *grads_hi], count, True
    )
    keep_second, send_second, pg_second, pg_second_other = out_terms(
        block_second, hiddens_hi, [to_mid[0], *grads_mid], count, False
    )
    out_first = [keep_first] + [along_hi(value, -s) for s, value in enumerate(send_first, 1)]
    out_second = [keep_second] + [along_mid(value, -t) for t, value in enumerate(send_second, 1)]
    out_own, out_other = summed_halves(out_first, out_second)
    block_out = to_raw(out_own, to_core(out_other), count, planes, rows)

    pg_first = pg_first + to_core(pg_first_other)
    pg_second = pg_second + to_core(pg_second_other)
    pg = jnp.zeros((chans, his, mids, 2 * chans), F32)
    for s in range(his):
        piece = pg_first[s * chans : (s + 1) * chans]
        if s:
            piece = along_hi(piece, -s)
        piece = piece.reshape(chans, 1, mids, 2 * chans)
        pg = lax.dynamic_update_slice_in_dim(pg, piece, (place.hi + s) % his, 1)
    pg_more = jnp.zeros((chans, his, mids, 2 * chans), F32)
    for t in range(mids):
        piece = pg_second[t * chans : (t + 1) * chans]
        if t:
            piece = along_mid(piece, -t)
        piece = piece.reshape(chans, his, 1, 2 * chans)
        pg_more = lax.dynamic_update_slice_in_dim(pg_more, piece, (place.mid + t) % mids, 2)
    pg = (pg + pg_more).reshape(chans, -1)

    taps = tap_gradient(cells, image_up, image_down, back_own, back_arrived, count, planes, rows)[0]
    input_grad = input_gradient(back_own, back_arrived, back_up, back_down, depth_filter, count, planes, rows)

    slab = lax.axis_index("space")
    apart = slabs // 2
    while apart:
        low, high = jnp.split(pg, 2, axis=1)
        upper = (slab & apart) != 0
        pairs = [(i, i ^ apart) for i in range(slabs)]
        pg = jnp.where(upper, high, low) + lax.ppermute(jnp.where(upper, low, high), "space", pairs)
        taps = taps + lax.ppermute(taps, "space", pairs)
        apart //= 2
    return block_out, pg * grad_scale, input_grad, taps.reshape(27, chans) * grad_scale


def solution(mesh):
    placed = (
        P("chan", None, "space", None),
        P(None, "chan"),
        P("chan", None),
        P("chan", None, "space", None),
    )
    return jax.shard_map(
        body,
        mesh=mesh,
        in_specs=placed,
        out_specs=(
            P("chan", None, "space", None),
            P("chan", "space"),
            P("chan", None, "space", None),
            P(None, "chan"),
        ),
        check_vma=False,
    )
```

```python
import math

import jax
import jax.numpy as jnp
from jax import lax
from jax.experimental import pallas as pl
from jax.experimental.pallas import tpu as pltpu
from jax.sharding import PartitionSpec as P

F32, BF16 = jnp.float32, jnp.bfloat16
HINTS = dict(
    inner=0.1, outer=20, back=0.1, out=0.1, filter=0.1, sums=0.1, out_sums=0.1, taps=0.1, late_taps=0.1, input=20, pack=0.1, last=0.1
)
RATE = 10**9
IN_VMEM = pl.BlockSpec(memory_space=pltpu.VMEM)
ANYWHERE = pl.BlockSpec(memory_space=pl.ANY)


class Place:
    def __init__(self, count):
        self.mids = 2
        self.his = count // 4
        index = lax.axis_index("chan")
        self.core = index % 2
        self.mid = index // 2 % self.mids
        self.hi = index // 2 // self.mids

    def block(self, hi_back, mid_back, core_flip):
        hi = (self.hi + self.his - hi_back) % self.his
        mid = (self.mid + self.mids - mid_back) % self.mids
        core = 1 - self.core if core_flip else self.core
        return hi, mid, core

    def flat(self, hi, mid, core):
        return (hi * self.mids + mid) * 2 + core


def size_of(shape, dtype):
    return math.prod(shape) * jnp.dtype(dtype).itemsize


def rims(near, far):
    odd = lax.axis_index("space") % 2 == 1

    def up(p):
        return jnp.where(odd, near[p].astype(F32), far[p].astype(F32))

    def down(p):
        return jnp.where(odd, far[p].astype(F32), near[p].astype(F32))

    return up, down


def kernel_call(kernel, outs, args, scratch=(), after=(), micros=0.1, places=None):
    used = len(args)

    def run(*refs):
        kernel(*refs[:used], *refs[used + len(after) :])

    held = [x for x in (*args, *outs, *scratch) if jnp.issubdtype(x.dtype, jnp.floating)]
    room = sum(size_of(x.shape, x.dtype) for x in held)
    return pl.pallas_call(
        run,
        out_shape=outs,
        in_specs=[IN_VMEM] * used + [ANYWHERE] * len(after),
        out_specs=places or [IN_VMEM] * len(outs),
        scratch_shapes=list(scratch),
        compiler_params=pltpu.CompilerParams(vmem_limit_bytes=room + 4 * 2**20),
        cost_estimate=pl.CostEstimate(flops=int(micros * RATE), bytes_accessed=0, transcendentals=0),
    )(*args, *after)


def shaped(shape, dtype=BF16):
    return jax.ShapeDtypeStruct(shape, dtype)


def line_home(line, rows):
    plane, row = divmod(line, rows)
    quarter = rows // 4
    core = row // (2 * quarter)
    outer = (row // quarter) in (0, 3)
    return core, outer, plane * quarter + row % quarter


def raw_to_cells(raw, chans, store):
    lines = raw.shape[0] // chans

    @pl.loop(0, chans // 16)
    def _(g):
        group = pl.ds(pl.multiple_of(g * 16, 16), 16)
        for first in range(0, lines, 16):
            block = [raw[pl.ds(pl.multiple_of((g * 16 + c) * lines + first, 16), 16), :] for c in range(16)]
            turned = jnp.swapaxes(jnp.stack([b.astype(F32) for b in block]), 0, 1).astype(BF16)
            for i in range(16):
                store(first + i, group, turned[i])


def write_raw(load, raw, room, sems, chans, lines):
    def copy(start):
        rows = slice(start * lines, (start + 16) * lines)
        return pltpu.make_async_copy(room.at[rows], raw.at[rows], sems.at[start // 16])

    for start in range(0, chans, 16):
        group = slice(start, start + 16)
        for first in range(0, lines, 16):
            block = jnp.stack([load(first + i, group).astype(F32) for i in range(16)])
            turned = jnp.swapaxes(block, 0, 1).astype(BF16)
            for c in range(16):
                at = (start + c) * lines + first
                room[at : at + 16] = turned[c]
        copy(start).start()
    for start in range(0, chans, 16):
        copy(start).wait()


def relayout_images(images, after=()):
    chans, planes, rows, width = images.shape

    def kernel(raw, cells, near, far):
        odd = lax.axis_index("space") % 2 == 1

        def store(line, group, value):
            cells[line, group] = value

        raw_to_cells(raw, chans, store)
        for parity, (first, last) in enumerate(((far, near), (near, far))):

            @pl.when(odd == bool(parity))
            def _():
                @pl.loop(0, planes)
                def _(p):
                    first[p] = cells[p * rows]
                    last[p] = cells[p * rows + rows - 1]

    edge = shaped((planes, chans, width))
    return kernel_call(
        kernel,
        [shaped((planes * rows, chans, width)), edge, edge],
        [images.reshape(-1, width)],
        (),
        after,
    )


def relayout_grad(grad_out, count, after=()):
    chans, planes, rows, width = grad_out.shape
    half = planes * rows // 2

    def kernel(raw, own, other):
        core = Place(count).core
        for mine in range(2):

            @pl.when(core == mine)
            def _():
                def store(line, group, value):
                    home, outer, at = line_home(line, rows)
                    out = own if home == mine else other
                    out[outer * (half // 2) + at, group] = value

                raw_to_cells(raw, chans, store)

    part = shaped((half, chans, width))
    return kernel_call(kernel, [part, part], [grad_out.reshape(-1, width)], (), after, 0.5)


def tap_planes(weights, spread, chans, width):
    turned = jnp.concatenate([weights, jnp.zeros((5, chans), F32)], axis=0).T
    for k in range(27):
        spread[k] = jnp.broadcast_to(turned[:, k : k + 1], (chans, width))


def fill_window(padded, line, up, down, planes, rows):
    zero = jnp.zeros(padded.shape[1:], F32)
    for n in range(rows + 2):
        padded[n] = zero
        padded[(planes + 1) * (rows + 2) + n] = zero

    @pl.loop(0, planes)
    def _(p):
        base = (p + 1) * (rows + 2)
        if up is not None:
            padded[base] = up(p)
            padded[base + rows + 1] = down(p)
        for r in range(rows):
            padded[base + 1 + r] = line(p, r).astype(F32)


def depthwise(padded, spread, planes, rows, wanted, store, flipped):
    _, chans, width = padded.shape
    lane = lax.broadcasted_iota(jnp.int32, (8, width), 1)
    deep = 4 // len(wanted)

    def summed(first, group):
        sums = {(d, r): [None] * 3 for d in range(deep) for r in wanted}
        for a in range(3):
            taps = [[spread[26 - 9 * a - 3 * b - e if flipped else 9 * a + 3 * b + e, group] for e in range(3)] for b in range(3)]
            for d in range(deep):
                for line in sorted({r + b for r in wanted for b in range(3)}):
                    cells = padded[(first + d + a) * (rows + 2) + line, group]
                    for b in range(3):
                        if line - b in wanted:
                            held = sums[d, line - b]
                            for e in range(3):
                                term = taps[b][e] * cells
                                held[e] = term if held[e] is None else held[e] + term
        for place, held in sums.items():
            before = jnp.where(lane == 0, 0.0, pltpu.roll(held[0], 1, 1))
            after = jnp.where(lane == width - 1, 0.0, pltpu.roll(held[2], width - 1, 1))
            sums[place] = held[1] + before + after
        return sums

    @pl.loop(0, planes // deep)
    def _(i):
        for start in range(0, chans, 16):
            low = summed(i * deep, slice(start, start + 8))
            high = summed(i * deep, slice(start + 8, start + 16))
            for d, r in low:
                both = jnp.concatenate([low[d, r], high[d, r]], axis=0)
                store(i * deep + d, r, slice(start, start + 16), both)


def hidden_part(cells, up, down, weights, count, planes, rows, outer, after=()):
    _, chans, width = cells.shape
    quarter = rows // 4
    args = [cells, up, down, weights] if outer else [cells, weights]
    wanted = [r for r in range(rows) if ((r // quarter) in (0, 3)) == outer]

    def kernel(cells, *refs):
        weights, own, other, padded, spread, both = refs[-6:]
        up, down = rims(*refs[:2]) if outer else (None, None)
        core = Place(count).core
        tap_planes(weights[...], spread, chans, width)
        fill_window(
            padded,
            lambda p, r: cells[p * rows + r],
            up,
            down,
            planes,
            rows,
        )

        def put(p, r, group, value):
            home, _, at = line_home(r, rows)
            both[home, p * quarter + at, group] = value.astype(BF16)

        depthwise(padded, spread, planes, rows, wanted, put, False)

        @pl.loop(0, planes * quarter)
        def _(i):
            own[i] = both[core, i]
            other[i] = both[1 - core, i]

    part = shaped((planes * quarter, chans, width))
    return kernel_call(
        kernel,
        [part, part],
        args,
        [
            pltpu.VMEM(((planes + 2) * (rows + 2), chans, width), F32),
            pltpu.VMEM((27, chans, width), F32),
            pltpu.VMEM((2, planes * quarter, chans, width), BF16),
        ],
        after,
        HINTS["outer" if outer else "inner"],
    )


def picked(table, starts, chans):
    total, wide = table.shape[1], len(starts) * chans
    col = lax.broadcasted_iota(jnp.int32, (total, wide), 1)
    row = lax.broadcasted_iota(jnp.int32, (total, wide), 0)
    want = jnp.zeros((total, wide), jnp.int32)
    for b, start in enumerate(starts):
        want = jnp.where((col >= b * chans) & (col < (b + 1) * chans), start + col - b * chans, want)
    choice = jnp.where(row == want, 1.0, 0.0).astype(BF16)
    return jnp.dot(table, choice, preferred_element_type=F32).astype(BF16)


def pack_grad(own, arrived, filter_own, filter_arrived, count, after=()):
    half, chans, width = own.shape
    part = half // 2
    his, mids = count // 4, 2
    hi_slices, mid_slices = mids * 2 * chans // width, his * 2 * chans // width

    def kernel(own, arrived, filter_own, filter_arrived, *outs):
        place = Place(count)
        table = jnp.concatenate([filter_own[...], filter_arrived[...]], axis=0)
        to_hi, to_mid = outs[: his - 1], outs[his - 1 : his + mids - 2]
        mine_hi, mine_mid = outs[-2:]

        def columns(for_hi, hi, mid):
            if for_hi:
                cells = [(hi, (mid + mids - t) % mids) for t in range(mids)]
            else:
                cells = [((hi + his - s) % his, mid) for s in range(his)]
            starts = [
                place.flat(hi_, mid_, place.core if q == 0 else 1 - place.core) * chans
                for hi_, mid_ in cells
                for q in range(2)
            ]
            return picked(table, starts, chans)

        def put(out, base, value):
            for i in range(value.shape[1] // width):
                out[base + i] = value[:, i * width : (i + 1) * width]

        for refs, offset in ((to_hi, 0), (to_mid, part)):

            @pl.loop(0, part)
            def _(i):
                for ref in refs:
                    ref[i, :chans] = own[offset + i]
                    ref[i, chans:] = arrived[offset + i]

        for s, ref in enumerate(to_hi, 1):
            put(ref, part, columns(True, (place.hi + s) % his, place.mid))
        for t, ref in enumerate(to_mid, 1):
            put(ref, part, columns(False, place.hi, (place.mid + t) % mids))
        put(mine_hi, 0, columns(True, place.hi, place.mid))
        put(mine_mid, 0, columns(False, place.hi, place.mid))

    outs = (
        [shaped((part + hi_slices, 2 * chans, width))] * (his - 1)
        + [shaped((part + mid_slices, 2 * chans, width))] * (mids - 1)
        + [shaped((hi_slices, 2 * chans, width)), shaped((mid_slices, 2 * chans, width))]
    )
    outs = kernel_call(kernel, outs, [own, arrived, filter_own, filter_arrived], (), after, micros=HINTS["pack"])
    return outs[: his - 1], outs[his - 1 : his + mids - 2], outs[-2], outs[-1]


def product_terms(weights, blocks, outs, part, both, width):
    step = math.gcd(part, 4)

    @pl.loop(0, part // step)
    def _(i):
        cells = jnp.concatenate(
            [jnp.concatenate([ref[i * step + j] for ref in blocks], axis=0) for j in range(step)], axis=1
        )
        product = jnp.dot(weights, cells, preferred_element_type=F32).astype(BF16)
        for n, out in enumerate(outs):
            for j in range(step):
                out[i * step + j] = product[n * both : (n + 1) * both, j * width : (j + 1) * width]


def back_terms(parts, after=()):
    args, outs, plans = [], [], []
    for mine, arrived, filter_mine, sends in parts:
        slices, both, width = filter_mine.shape
        part = mine.shape[0] - slices
        plans.append((len(args), len(outs), len(arrived), sends, slices, part))
        args += [mine, filter_mine, *arrived]
        outs += [shaped((part, both, width))] * (sends + 1) + [shaped(((1 + len(arrived)) * both, slices * width))]
    used = len(args)

    def kernel(*refs):
        for start, out, many, sends, slices, part in plans:
            mine, filter_mine, *arrived = refs[start : start + 2 + many]
            rows = [jnp.concatenate([filter_mine[i] for i in range(slices)], axis=1)]
            for ref in arrived:
                rows.append(jnp.concatenate([ref[part + i] for i in range(slices)], axis=1))
            block = jnp.concatenate(rows, axis=0)
            refs[used + out + sends + 1][...] = block
            turned = block.astype(F32).T.astype(BF16)
            product_terms(turned, [mine, *arrived], refs[used + out : used + out + sends + 1], part, both, width)

    done = kernel_call(kernel, outs, args, (), after, micros=HINTS["back"])
    return [(done[o], done[o + 1 : o + 1 + sends], done[o + 1 + sends]) for _, o, _, sends, _, _ in plans]


def summed_parts(first, second, after=(), name="sums"):
    part, both, width = first[0].shape
    chans = both // 2

    def kernel(*refs):
        outs = refs[-4:]
        for n, terms in enumerate((refs[: len(first)], refs[len(first) : -4])):

            @pl.loop(0, part)
            def _(i):
                total = terms[0][i].astype(F32)
                for term in terms[1:]:
                    total = total + term[i].astype(F32)
                outs[n][i] = total[:chans].astype(BF16)
                outs[2 + n][i] = total[chans:].astype(BF16)

    done = kernel_call(kernel, [shaped((part, chans, width))] * 4, [*first, *second], (), after, HINTS[name])
    return done[:2], done[2:]


def edge_rows(own, arrived, count, rows, after=()):
    part, chans, width = own.shape
    quarter = rows // 4
    planes = part // quarter

    def kernel(own, arrived, near, far):
        core = Place(count).core
        odd = lax.axis_index("space") % 2
        for mine in range(2):
            for parity in range(2):

                @pl.when((core == mine) & (odd == parity))
                def _():
                    first, last = (own, arrived) if mine == 0 else (arrived, own)
                    to_first, to_last = (near, far) if parity else (far, near)

                    @pl.loop(0, planes)
                    def _(p):
                        to_first[p] = first[p * quarter]
                        to_last[p] = last[p * quarter + quarter - 1]

    edge = shaped((planes, chans, width))
    return kernel_call(kernel, [edge, edge], [own, arrived], (), after)


def joined(own, arrived, after=()):
    part, chans, width = own[0].shape
    many = len(own)

    def kernel(*refs):
        @pl.loop(0, part)
        def _(i):
            for a, b, out in zip(refs[:many], refs[many : 2 * many], refs[2 * many :]):
                out[i, :chans] = a[i]
                out[i, chans:] = b[i]

    return kernel_call(kernel, [shaped((part, 2 * chans, width))] * many, [*own, *arrived], (), after)


def out_terms(parts, after=()):
    args, outs, plans = [], [], []
    for block, hiddens, terms in parts:
        plans.append((len(args), len(outs), len(hiddens), terms))
        args += [block, *hiddens]
        outs += [shaped(hiddens[0].shape)] * terms
    used = len(args)

    def kernel(*refs):
        for start, out, many, terms in plans:
            part, both, width = refs[start + 1].shape
            product_terms(
                refs[start][...],
                refs[start + 1 : start + 1 + many],
                refs[used + out : used + out + terms],
                part,
                both,
                width,
            )

    done = kernel_call(kernel, outs, args, (), after, micros=HINTS["out"])
    return [done[o : o + terms] for _, o, _, terms in plans]


def filter_terms(parts, count, after=()):
    args, plans, outs, scratch = [], [], [], []
    for hiddens, grads, over_mid in parts:
        part, both, width = hiddens[0].shape
        chans = both // 2
        plans.append((len(args), len(outs), len(hiddens), len(grads), over_mid))
        args += [*hiddens, *grads]
        outs += [shaped((both, len(hiddens) * both), F32)] * len(grads)
        scratch += [
            pltpu.VMEM((len(hiddens) * both, part * width), BF16),
            pltpu.VMEM((len(grads) * both, part * width), BF16),
        ]
    used = len(args)

    def kernel(*refs):
        place = Place(count)
        results, rooms = refs[used : used + len(outs)], refs[used + len(outs) :]
        for n, (start, out, cols_of, rows_of, over_mid) in enumerate(plans):
            hidden = refs[start : start + cols_of]
            grad = refs[start + cols_of : start + cols_of + rows_of]
            ordered, lined = rooms[2 * n], rooms[2 * n + 1]
            for j in range(part):
                span = slice(j * width, (j + 1) * width)
                for i, ref in enumerate(hidden):
                    hi, mid, _ = place.block(0, i, 0) if over_mid else place.block(i, 0, 0)
                    for q in range(2):
                        core = 1 - place.core if q else place.core
                        at = pl.multiple_of(((mid if over_mid else hi) * 2 + core) * chans, chans)
                        ordered[pl.ds(at, chans), span] = ref[j, q * chans : (q + 1) * chans]
                for i, ref in enumerate(grad):
                    lined[i * both : (i + 1) * both, span] = ref[j]
            pairs = lax.dot_general(lined[...], ordered[...], (((1,), (1,)), ((), ())), preferred_element_type=F32)
            for i in range(rows_of):
                results[out + i][...] = pairs[i * both : (i + 1) * both]

    done = kernel_call(kernel, outs, args, scratch, after, HINTS["filter"])
    return [done[out : out + rows_of] for _, out, _, rows_of, _ in plans]


def filter_gathered(for_hi, for_mid, count, after=()):
    his, mids = len(for_hi), len(for_mid)
    chans, wide = for_hi[0].shape[0] // 2, for_hi[0].shape[1]
    pair = wide // mids

    def kernel(*refs):
        place = Place(count)

        def chosen(pieces, at, mine):
            value = pieces[0][...]
            for n, piece in enumerate(pieces[1:], 1):
                value = jnp.where((mine + n) % len(pieces) == at, piece[...], value)
            return value

        by_hi = [chosen(refs[:his], hi, place.hi) for hi in range(his)]
        by_mid = [chosen(refs[his : his + mids], mid, place.mid) for mid in range(mids)]
        for hi in range(his):
            for mid in range(mids):
                block = by_hi[hi][:, mid * pair : (mid + 1) * pair] + by_mid[mid][:, hi * pair : (hi + 1) * pair]
                at = (hi * mids + mid) * chans
                refs[-2][at : at + chans] = block[:chans]
                refs[-1][at : at + chans] = block[chans:]

    out = shaped((his * mids * chans, pair), F32)
    return kernel_call(kernel, [out, out], [*for_hi, *for_mid], (), after)


def slab_pieces(own, arrived, taps, slabs, after=()):
    rows = own.shape[0] // slabs
    wide = own.shape[1]

    def kernel(own, arrived, taps, *outs):
        slab = lax.axis_index("space")
        for apart, out in enumerate(outs):
            at = pl.ds(pl.multiple_of(jnp.bitwise_xor(slab, apart) * rows, rows), rows)
            out[:rows] = own[at] + arrived[at]
            out[rows:] = taps[...]

    piece = shaped((rows + taps.shape[0], wide), F32)
    return kernel_call(kernel, [piece] * slabs, [own, arrived, taps], (), after)


def last_outputs(own, arrived, pieces, count, planes, rows, scale, after=()):
    _, chans, width = own[0].shape
    lines, many = planes * rows, len(pieces)

    def kernel(*refs):
        raw, filter_out, tap_out, room, sems = refs[4 + many :]
        core = Place(count).core
        for mine in range(2):

            @pl.when(core == mine)
            def _():
                def load(line, group):
                    home, outer, at = line_home(line, rows)
                    return refs[outer if home == mine else 2 + outer][at, group]

                write_raw(load, raw, room, sems, chans, lines)

        total = refs[4][...]
        for ref in refs[5 : 4 + many]:
            total = total + ref[...]
        total = total * scale
        filter_out[...] = total[:chans]
        tap_out[...] = total[chans : chans + 27, :chans]

    outs = [
        shaped((chans * lines, width)),
        shaped((chans, pieces[0].shape[1]), F32),
        shaped((27, chans), F32),
    ]
    scratch = [pltpu.VMEM((chans * lines, width), BF16), pltpu.SemaphoreType.DMA((chans // 16,))]
    raw, filter_out, tap_out = kernel_call(
        kernel, outs, [*own, *arrived, *pieces], scratch, after, HINTS["last"], [ANYWHERE, IN_VMEM, IN_VMEM]
    )
    return raw.reshape(chans, planes, rows, width), filter_out, tap_out


def input_gradient(own, arrived, near, far, weights, count, planes, rows, after=()):
    _, chans, width = own[0].shape
    quarter, lines = rows // 4, planes * rows

    def kernel(*refs):
        own, arrived = refs[:2], refs[2:4]
        near, far, weights, raw, token, padded, spread, cells, room, sems = refs[4:]
        core = Place(count).core
        token[...] = jnp.zeros(token.shape, F32)
        tap_planes(weights[...], spread, chans, width)

        def line(p, r):
            home, outer, at = line_home(r, rows)
            place = p * quarter + at
            return jnp.where(core == home, own[outer][place].astype(F32), arrived[outer][place].astype(F32))

        fill_window(padded, line, *rims(near, far), planes, rows)

        def store(p, r, group, value):
            cells[p * rows + r, group] = value.astype(BF16)

        depthwise(padded, spread, planes, rows, list(range(rows)), store, True)
        write_raw(lambda line, group: cells[line, group], raw, room, sems, chans, lines)

    raw, token = kernel_call(
        kernel,
        [shaped((chans * lines, width)), shaped((8, width), F32)],
        [*own, *arrived, near, far, weights],
        [
            pltpu.VMEM(((planes + 2) * (rows + 2), chans, width), F32),
            pltpu.VMEM((27, chans, width), F32),
            pltpu.VMEM((lines, chans, width), BF16),
            pltpu.VMEM((chans * lines, width), BF16),
            pltpu.SemaphoreType.DMA((chans // 16,)),
        ],
        after,
        HINTS["input"],
        [ANYWHERE, IN_VMEM],
    )
    return raw.reshape(chans, planes, rows, width), token


def tap_sums(cells, up, down, back, before, count, planes, rows, others, wide, after=()):
    _, chans, width = cells.shape
    half, quarter = rows // 2, rows // 4
    last = before is not None
    args = [cells, up, down, *back] + ([before] if last else [])

    def kernel(cells, near, far, inner, outside, *refs):
        out, padded, back = refs[-3 - last : len(refs) - last]
        sums = refs[-1] if last else out
        core = Place(count).core
        home = 1 - core if others else core
        fill_window(padded, lambda p, r: cells[p * rows + r], *rims(near, far), planes, rows)
        sums[...] = refs[0][...] if last else jnp.zeros(sums.shape, F32)
        lane = lax.broadcasted_iota(jnp.int32, (8, width), 1)
        deep = max(1, 4 // half)

        @pl.loop(0, planes * quarter)
        def _(i):
            back[0, i] = jnp.where(home == 0, outside[i].astype(F32), inner[i].astype(F32))
            back[1, i] = jnp.where(home == 0, inner[i].astype(F32), outside[i].astype(F32))

        @pl.loop(0, planes // deep)
        def _(i):
            for pair in range(0, chans, 16):
                both = {}
                for d in range(deep):
                    for r in range(half):
                        place = (i * deep + d) * quarter + r % quarter
                        both[d, r] = back[r // quarter, place, pair : pair + 16]
                for n in range(2):
                    group = slice(pair + 8 * n, pair + 8 * n + 8)
                    moved = {}
                    for key, value in both.items():
                        here = value[8 * n : 8 * n + 8]
                        later = jnp.where(lane == width - 1, 0.0, pltpu.roll(here, width - 1, 1))
                        earlier = jnp.where(lane == 0, 0.0, pltpu.roll(here, 1, 1))
                        moved[key] = (later, here, earlier)
                    for a in range(3):
                        images = {}
                        for d in range(deep):
                            base = (i * deep + d + a) * (rows + 2) + home * half
                            for line in range(half + 2):
                                images[d, line] = padded[base + line, group]
                        for b in range(3):
                            for e in range(3):
                                term = None
                                for (d, r), values in moved.items():
                                    product = images[d, r + b] * values[e]
                                    term = product if term is None else term + product
                                sums[9 * a + 3 * b + e, group] += term

        if last:
            row = lax.broadcasted_iota(jnp.int32, (chans, wide), 0)
            col = lax.broadcasted_iota(jnp.int32, (chans, wide), 1)
            for tap in range(27):
                total = jnp.sum(sums[tap], axis=1, keepdims=True)
                out[tap : tap + 1] = jnp.sum(jnp.where(row == col, total, 0.0), axis=0, keepdims=True)
            out[27:] = jnp.zeros((5, wide), F32)

    running = (27, chans, width)
    scratch = [
        pltpu.VMEM(((planes + 2) * (rows + 2), chans, width), F32),
        pltpu.VMEM((2, planes * quarter, chans, width), F32),
    ]
    if last:
        scratch.append(pltpu.VMEM(running, F32))
    outs = [shaped((32, wide) if last else running, F32)]
    return kernel_call(kernel, outs, args, scratch, after, HINTS["late_taps" if last else "taps"])[0]


def body(images, depth_filter, point_filter, grad_out):
    chans, planes, rows, width = images.shape
    count, slabs = lax.axis_size("chan"), lax.axis_size("space")
    his, mids = count // 4, 2
    place = Place(count)
    grad_scale = 1.0 / math.sqrt(planes * rows * width * slabs)

    def moved(value, target):
        pairs = []
        for i in range(count):
            hi, mid, core = target(i // 2 // mids, i // 2 % mids, i % 2)
            pairs.append((i, (hi % his * mids + mid % mids) * 2 + core))
        return lax.ppermute(value, "chan", pairs)

    def to_core(value):
        return moved(value, lambda hi, mid, core: (hi, mid, 1 - core))

    def along_hi(value, by):
        return moved(value, lambda hi, mid, core: (hi + by, mid, core))

    def along_mid(value, by):
        return moved(value, lambda hi, mid, core: (hi, mid + by, core))

    def halo(near, far):
        swaps = [[(i + d, i + 1 - d) for i in range(first, slabs - 1, 2) for d in range(2)] for first in range(2)]
        return lax.ppermute(near, "space", swaps[0]), lax.ppermute(far, "space", swaps[1])

    def exchanged(value, apart):
        return lax.ppermute(value, "space", [(i, i ^ apart) for i in range(slabs)])

    filter_arrived = to_core(point_filter)
    grad_own, grad_other = relayout_grad(grad_out, count)
    grad_arrived = to_core(grad_other)
    cells, near, far = relayout_images(images, [grad_own])
    image_rims = halo(near, far)
    to_hi, to_mid, filter_hi, filter_mid = pack_grad(
        grad_own, grad_arrived, point_filter, filter_arrived, count, [cells]
    )
    grads_hi = [along_hi(value, s) for s, value in enumerate(to_hi, 1)]
    grads_mid = [along_mid(value, t) for t, value in enumerate(to_mid, 1)]

    windows = (cells, *image_rims)
    plan = (count, planes, rows)
    inner_own, inner_other = hidden_part(*windows, depth_filter, *plan, False, [to_hi[0]])
    inner_arrived = to_core(inner_other)
    (keep_first, send_first, block_first), (keep_second, send_second, block_second) = back_terms(
        [(to_hi[0], grads_hi, filter_hi, mids - 1), (to_mid[0], grads_mid, filter_mid, his - 1)], [inner_own]
    )
    back_first = [keep_first] + [along_mid(value, -t) for t, value in enumerate(send_first, 1)]
    back_second = [keep_second] + [along_hi(value, -s) for s, value in enumerate(send_second, 1)]

    outer_own, outer_other = hidden_part(*windows, depth_filter, *plan, True, [keep_first])
    outer_arrived = to_core(outer_other)
    hidden_first, hidden_second = joined([inner_own, outer_own], [inner_arrived, outer_arrived])
    hiddens_mid = [hidden_first] + [along_mid(hidden_first, t) for t in range(1, mids)]
    hiddens_hi = [hidden_second] + [along_hi(hidden_second, s) for s in range(1, his)]

    back_own, back_other = summed_parts(back_first, back_second, [hidden_first])
    back_arrived = [to_core(value) for value in back_other]
    wide = his * mids * 2 * chans // slabs
    taps = tap_sums(*windows, back_own, None, *plan, False, wide, [back_own[0]])
    edges = edge_rows(back_own[1], back_arrived[1], count, rows, [taps])
    back_rims = halo(*edges)

    for_hi, for_mid = filter_terms(
        [(hiddens_mid, [to_hi[0], *grads_hi], True), (hiddens_hi, [to_mid[0], *grads_mid], False)], count, [edges[0]]
    )
    owned = for_hi[0]
    for_hi = [for_hi[0]] + [along_hi(piece, -s) for s, piece in enumerate(for_hi[1:], 1)]
    for_mid = [for_mid[0]] + [along_mid(piece, -t) for t, piece in enumerate(for_mid[1:], 1)]
    out_first, out_second = out_terms(
        [(block_first, hiddens_mid, his), (block_second, hiddens_hi, mids)], [owned]
    )
    latest = out_first[0]
    out_first = [out_first[0]] + [along_hi(value, -s) for s, value in enumerate(out_first[1:], 1)]
    out_second = [out_second[0]] + [along_mid(value, -t) for t, value in enumerate(out_second[1:], 1)]

    input_grad, latest = input_gradient(back_own, back_arrived, *back_rims, depth_filter, *plan, [latest])
    taps = tap_sums(*windows, back_arrived, taps, *plan, True, wide, [latest])
    own, other = filter_gathered(for_hi, for_mid, count, [taps])
    chip_arrived = to_core(other)
    if own.shape[1] != wide:

        def by_slab(value):
            value = value.reshape(his * mids, chans, -1).swapaxes(0, 1).reshape(chans, slabs, wide)
            return value.swapaxes(0, 1).reshape(-1, wide)

        own, chip_arrived = by_slab(own), by_slab(chip_arrived)
    pieces = slab_pieces(own, chip_arrived, taps, slabs)
    latest = pieces[0]
    pieces = [pieces[0]] + [exchanged(piece, apart) for apart, piece in enumerate(pieces[1:], 1)]
    out_own, out_other = summed_parts(out_first, out_second, [latest], "out_sums")
    out_arrived = [to_core(value) for value in out_other]
    block_out, point_grad, depth_grad = last_outputs(out_own, out_arrived, pieces, *plan, grad_scale)
    return block_out, point_grad, input_grad, depth_grad


def solution(mesh):
    placed = (
        P("chan", None, "space", None),
        P(None, "chan"),
        P("chan", None),
        P("chan", None, "space", None),
    )
    return jax.shard_map(
        body,
        mesh=mesh,
        in_specs=placed,
        out_specs=(
            P("chan", None, "space", None),
            P("chan", "space"),
            P("chan", None, "space", None),
            P(None, "chan"),
        ),
        check_vma=False,
    )
```

```python
import math

import jax
import jax.numpy as jnp
from jax import lax
from jax.experimental import pallas as pl
from jax.experimental.pallas import tpu as pltpu
from jax.sharding import PartitionSpec as P

F32, BF16 = jnp.float32, jnp.bfloat16
HINTS = dict(
    inner=0.1, outer=0.1, back=0.1, out=0.1, sums=0.1, out_sums=0.1, taps=0.1, late_taps=0.1, input=20, pack=0.1, last=0.1, relayout=1.5
)
RATE = 10**9
IN_VMEM = pl.BlockSpec(memory_space=pltpu.VMEM)
ANYWHERE = pl.BlockSpec(memory_space=pl.ANY)


class Place:
    def __init__(self, count):
        self.mids = 2
        self.his = count // 4
        index = lax.axis_index("chan")
        self.core = index % 2
        self.mid = index // 2 % self.mids
        self.hi = index // 2 // self.mids

    def block(self, hi_back, mid_back, core_flip):
        hi = (self.hi + self.his - hi_back) % self.his
        mid = (self.mid + self.mids - mid_back) % self.mids
        core = 1 - self.core if core_flip else self.core
        return hi, mid, core

    def flat(self, hi, mid, core):
        return (hi * self.mids + mid) * 2 + core


def size_of(shape, dtype):
    return math.prod(shape) * jnp.dtype(dtype).itemsize


def rims(near, far):
    odd = lax.axis_index("space") % 2 == 1

    def up(p):
        return jnp.where(odd, near[p].astype(F32), far[p].astype(F32))

    def down(p):
        return jnp.where(odd, far[p].astype(F32), near[p].astype(F32))

    return up, down


def kernel_call(kernel, outs, args, scratch=(), after=(), micros=0.1, places=None):
    used = len(args)

    def run(*refs):
        kernel(*refs[:used], *refs[used + len(after) :])

    held = [x for x in (*args, *outs, *scratch) if jnp.issubdtype(x.dtype, jnp.floating)]
    room = sum(size_of(x.shape, x.dtype) for x in held)
    return pl.pallas_call(
        run,
        out_shape=outs,
        in_specs=[IN_VMEM] * used + [ANYWHERE] * len(after),
        out_specs=places or [IN_VMEM] * len(outs),
        scratch_shapes=list(scratch),
        compiler_params=pltpu.CompilerParams(vmem_limit_bytes=room + 4 * 2**20),
        cost_estimate=pl.CostEstimate(flops=int(micros * RATE), bytes_accessed=0, transcendentals=0),
    )(*args, *after)


def shaped(shape, dtype=BF16):
    return jax.ShapeDtypeStruct(shape, dtype)


def line_home(line, rows):
    plane, row = divmod(line, rows)
    quarter = rows // 4
    core = row // (2 * quarter)
    outer = (row // quarter) in (0, 3)
    return core, outer, plane * quarter + row % quarter


def raw_to_cells(raw, chans, store):
    lines = raw.shape[0] // chans

    @pl.loop(0, chans // 16)
    def _(g):
        group = pl.ds(pl.multiple_of(g * 16, 16), 16)
        for first in range(0, lines, 16):
            block = [raw[pl.ds(pl.multiple_of((g * 16 + c) * lines + first, 16), 16), :] for c in range(16)]
            turned = jnp.swapaxes(jnp.stack([b.astype(F32) for b in block]), 0, 1).astype(BF16)
            for i in range(16):
                store(first + i, group, turned[i])


def write_raw(load, raw, room, sems, chans, lines):
    def copy(start):
        rows = slice(start * lines, (start + 16) * lines)
        return pltpu.make_async_copy(room.at[rows], raw.at[rows], sems.at[start // 16])

    for start in range(0, chans, 16):
        group = slice(start, start + 16)
        for first in range(0, lines, 16):
            block = jnp.stack([load(first + i, group).astype(F32) for i in range(16)])
            turned = jnp.swapaxes(block, 0, 1).astype(BF16)
            for c in range(16):
                at = (start + c) * lines + first
                room[at : at + 16] = turned[c]
        copy(start).start()
    for start in range(0, chans, 16):
        copy(start).wait()


def relayout_images(images, after=()):
    chans, planes, rows, width = images.shape

    def kernel(raw, cells, near, far):
        odd = lax.axis_index("space") % 2 == 1

        def store(line, group, value):
            cells[line, group] = value

        raw_to_cells(raw, chans, store)
        for parity, (first, last) in enumerate(((far, near), (near, far))):

            @pl.when(odd == bool(parity))
            def _():
                @pl.loop(0, planes)
                def _(p):
                    first[p] = cells[p * rows]
                    last[p] = cells[p * rows + rows - 1]

    edge = shaped((planes, chans, width))
    return kernel_call(
        kernel,
        [shaped((planes * rows, chans, width)), edge, edge],
        [images.reshape(-1, width)],
        (),
        after,
        HINTS["relayout"],
    )


def relayout_grad(grad_out, count, after=()):
    chans, planes, rows, width = grad_out.shape
    half = planes * rows // 2

    def kernel(raw, own, other):
        core = Place(count).core
        for mine in range(2):

            @pl.when(core == mine)
            def _():
                def store(line, group, value):
                    home, outer, at = line_home(line, rows)
                    out = own if home == mine else other
                    out[outer * (half // 2) + at, group] = value

                raw_to_cells(raw, chans, store)

    part = shaped((half, chans, width))
    return kernel_call(kernel, [part, part], [grad_out.reshape(-1, width)], (), after, HINTS["relayout"])


def tap_planes(weights, spread, chans, width):
    turned = jnp.concatenate([weights, jnp.zeros((5, chans), F32)], axis=0).T
    for k in range(27):
        spread[k] = jnp.broadcast_to(turned[:, k : k + 1], (chans, width))


def fill_window(padded, line, up, down, planes, rows):
    zero = jnp.zeros(padded.shape[1:], F32)
    for n in range(rows + 2):
        padded[n] = zero
        padded[(planes + 1) * (rows + 2) + n] = zero

    @pl.loop(0, planes)
    def _(p):
        base = (p + 1) * (rows + 2)
        if up is not None:
            padded[base] = up(p)
            padded[base + rows + 1] = down(p)
        for r in range(rows):
            padded[base + 1 + r] = line(p, r).astype(F32)


def depthwise(padded, spread, planes, rows, wanted, store, flipped):
    _, chans, width = padded.shape
    lane = lax.broadcasted_iota(jnp.int32, (8, width), 1)
    deep = 4 // len(wanted)

    def summed(first, group):
        sums = {(d, r): [None] * 3 for d in range(deep) for r in wanted}
        for a in range(3):
            taps = [[spread[26 - 9 * a - 3 * b - e if flipped else 9 * a + 3 * b + e, group] for e in range(3)] for b in range(3)]
            for d in range(deep):
                for line in sorted({r + b for r in wanted for b in range(3)}):
                    cells = padded[(first + d + a) * (rows + 2) + line, group]
                    for b in range(3):
                        if line - b in wanted:
                            held = sums[d, line - b]
                            for e in range(3):
                                term = taps[b][e] * cells
                                held[e] = term if held[e] is None else held[e] + term
        for place, held in sums.items():
            before = jnp.where(lane == 0, 0.0, pltpu.roll(held[0], 1, 1))
            after = jnp.where(lane == width - 1, 0.0, pltpu.roll(held[2], width - 1, 1))
            sums[place] = held[1] + before + after
        return sums

    @pl.loop(0, planes // deep)
    def _(i):
        for start in range(0, chans, 16):
            low = summed(i * deep, slice(start, start + 8))
            high = summed(i * deep, slice(start + 8, start + 16))
            for d, r in low:
                both = jnp.concatenate([low[d, r], high[d, r]], axis=0)
                store(i * deep + d, r, slice(start, start + 16), both)


def hidden_part(cells, near, far, weights, count, planes, rows, outer, after=()):
    _, chans, width = cells.shape
    quarter = rows // 4
    args = [cells, near, far, weights] if outer else [cells, weights]
    wanted = [r for r in range(rows) if ((r // quarter) in (0, 3)) == outer]

    def kernel(*refs):
        cells = refs[0]
        own, other, extra, both = refs[len(args) : len(args) + 4]
        core = Place(count).core
        if outer:
            padded, spread = extra, refs[3]
            up, down = rims(*refs[1:3])
        else:
            padded, spread = refs[-1], extra
            up, down = None, None
            tap_planes(refs[1][...], spread, chans, width)
        fill_window(padded, lambda p, r: cells[p * rows + r], up, down, planes, rows)

        def put(p, r, group, value):
            home, _, at = line_home(r, rows)
            both[home, p * quarter + at, group] = value.astype(BF16)

        depthwise(padded, spread, planes, rows, wanted, put, False)

        @pl.loop(0, planes * quarter)
        def _(i):
            own[i] = both[core, i]
            other[i] = both[1 - core, i]

    part = shaped((planes * quarter, chans, width))
    window = ((planes + 2) * (rows + 2), chans, width)
    outs = [part, part, shaped(window if outer else (27, chans, width), F32)]
    scratch = [pltpu.VMEM((2, planes * quarter, chans, width), BF16)]
    if not outer:
        scratch.append(pltpu.VMEM(window, F32))
    return kernel_call(kernel, outs, args, scratch, after, HINTS["outer" if outer else "inner"])


def picked(table, starts, chans):
    total, wide = table.shape[1], len(starts) * chans
    col = lax.broadcasted_iota(jnp.int32, (total, wide), 1)
    row = lax.broadcasted_iota(jnp.int32, (total, wide), 0)
    want = jnp.zeros((total, wide), jnp.int32)
    for b, start in enumerate(starts):
        want = jnp.where((col >= b * chans) & (col < (b + 1) * chans), start + col - b * chans, want)
    choice = jnp.where(row == want, 1.0, 0.0).astype(BF16)
    return jnp.dot(table, choice, preferred_element_type=F32).astype(BF16)


def pack_grad(own, arrived, filter_own, filter_arrived, count, after=()):
    half, chans, width = own.shape
    part = half // 2
    his, mids = count // 4, 2
    hi_slices, mid_slices = mids * 2 * chans // width, his * 2 * chans // width

    def kernel(own, arrived, filter_own, filter_arrived, *outs):
        place = Place(count)
        table = jnp.concatenate([filter_own[...], filter_arrived[...]], axis=0)
        to_hi, to_mid = outs[: his - 1], outs[his - 1 : his + mids - 2]
        mine_hi, mine_mid = outs[-2:]

        def columns(for_hi, hi, mid):
            if for_hi:
                cells = [(hi, (mid + mids - t) % mids) for t in range(mids)]
            else:
                cells = [((hi + his - s) % his, mid) for s in range(his)]
            starts = [
                place.flat(hi_, mid_, place.core if q == 0 else 1 - place.core) * chans
                for hi_, mid_ in cells
                for q in range(2)
            ]
            return picked(table, starts, chans)

        def put(out, base, value):
            for i in range(value.shape[1] // width):
                out[base + i] = value[:, i * width : (i + 1) * width]

        for refs, offset in ((to_hi, 0), (to_mid, part)):

            @pl.loop(0, part)
            def _(i):
                for ref in refs:
                    ref[i, :chans] = own[offset + i]
                    ref[i, chans:] = arrived[offset + i]

        for s, ref in enumerate(to_hi, 1):
            put(ref, part, columns(True, (place.hi + s) % his, place.mid))
        for t, ref in enumerate(to_mid, 1):
            put(ref, part, columns(False, place.hi, (place.mid + t) % mids))
        put(mine_hi, 0, columns(True, place.hi, place.mid))
        put(mine_mid, 0, columns(False, place.hi, place.mid))

    outs = (
        [shaped((part + hi_slices, 2 * chans, width))] * (his - 1)
        + [shaped((part + mid_slices, 2 * chans, width))] * (mids - 1)
        + [shaped((hi_slices, 2 * chans, width)), shaped((mid_slices, 2 * chans, width))]
    )
    outs = kernel_call(kernel, outs, [own, arrived, filter_own, filter_arrived], (), after, micros=HINTS["pack"])
    return outs[: his - 1], outs[his - 1 : his + mids - 2], outs[-2], outs[-1]


def product_terms(weights, blocks, outs, part, both, width):
    step = math.gcd(part, 4)

    @pl.loop(0, part // step)
    def _(i):
        cells = jnp.concatenate(
            [jnp.concatenate([ref[i * step + j] for ref in blocks], axis=0) for j in range(step)], axis=1
        )
        product = jnp.dot(weights, cells, preferred_element_type=F32).astype(BF16)
        for n, out in enumerate(outs):
            for j in range(step):
                out[i * step + j] = product[n * both : (n + 1) * both, j * width : (j + 1) * width]


def back_terms(parts, after=()):
    args, outs, plans = [], [], []
    for mine, arrived, filter_mine, sends in parts:
        slices, both, width = filter_mine.shape
        part = mine.shape[0] - slices
        plans.append((len(args), len(outs), len(arrived), sends, slices, part))
        args += [mine, filter_mine, *arrived]
        outs += [shaped((part, both, width))] * (sends + 1) + [shaped(((1 + len(arrived)) * both, slices * width))]
    used = len(args)

    def kernel(*refs):
        for start, out, many, sends, slices, part in plans:
            mine, filter_mine, *arrived = refs[start : start + 2 + many]
            rows = [jnp.concatenate([filter_mine[i] for i in range(slices)], axis=1)]
            for ref in arrived:
                rows.append(jnp.concatenate([ref[part + i] for i in range(slices)], axis=1))
            block = jnp.concatenate(rows, axis=0)
            refs[used + out + sends + 1][...] = block
            turned = block.astype(F32).T.astype(BF16)
            product_terms(turned, [mine, *arrived], refs[used + out : used + out + sends + 1], part, both, width)

    done = kernel_call(kernel, outs, args, (), after, micros=HINTS["back"])
    return [(done[o], done[o + 1 : o + 1 + sends], done[o + 1 + sends]) for _, o, _, sends, _, _ in plans]


def summed_parts(first, second, after=()):
    part, both, width = first[0].shape
    chans = both // 2

    def kernel(*refs):
        outs = refs[-4:]
        for n, terms in enumerate((refs[: len(first)], refs[len(first) : -4])):

            @pl.loop(0, part)
            def _(i):
                total = terms[0][i].astype(F32)
                for term in terms[1:]:
                    total = total + term[i].astype(F32)
                outs[n][i] = total[:chans].astype(BF16)
                outs[2 + n][i] = total[chans:].astype(BF16)

    done = kernel_call(kernel, [shaped((part, chans, width))] * 4, [*first, *second], (), after, HINTS["sums"])
    return done[:2], done[2:]


def edge_rows(own, arrived, count, rows, after=()):
    part, chans, width = own.shape
    quarter = rows // 4
    planes = part // quarter

    def kernel(own, arrived, near, far):
        core = Place(count).core
        odd = lax.axis_index("space") % 2
        for mine in range(2):
            for parity in range(2):

                @pl.when((core == mine) & (odd == parity))
                def _():
                    first, last = (own, arrived) if mine == 0 else (arrived, own)
                    to_first, to_last = (near, far) if parity else (far, near)

                    @pl.loop(0, planes)
                    def _(p):
                        to_first[p] = first[p * quarter]
                        to_last[p] = last[p * quarter + quarter - 1]

    edge = shaped((planes, chans, width))
    return kernel_call(kernel, [edge, edge], [own, arrived], (), after)


def joined(own, arrived, after=()):
    part, chans, width = own[0].shape
    many = len(own)

    def kernel(*refs):
        @pl.loop(0, part)
        def _(i):
            for a, b, out in zip(refs[:many], refs[many : 2 * many], refs[2 * many :]):
                out[i, :chans] = a[i]
                out[i, chans:] = b[i]

    return kernel_call(kernel, [shaped((part, 2 * chans, width))] * many, [*own, *arrived], (), after)


def out_terms(parts, count, after=()):
    args, plans, outs, scratch = [], [], [], []
    for block, hiddens, grads, over_mid in parts:
        part, both, width = hiddens[0].shape
        chans, wide = both // 2, len(hiddens) * both
        plans.append((len(args), len(outs), len(hiddens), len(grads), over_mid))
        args += [block, *hiddens, *grads]
        outs += [shaped((part, both, width)), shaped((both, wide), F32)]
        outs += [shaped((part + 2 * wide // width, both, width))] * (len(grads) - 1)
        scratch += [pltpu.VMEM((wide, part * width), BF16), pltpu.VMEM((len(grads) * both, part * width), BF16)]
    used = len(args)

    def kernel(*refs):
        place = Place(count)
        rooms = refs[used + len(outs) :]
        for n, (start, out, cols_of, rows_of, over_mid) in enumerate(plans):
            block, hidden = refs[start], refs[start + 1 : start + 1 + cols_of]
            grad = refs[start + 1 + cols_of : start + 1 + cols_of + rows_of]
            keep, gradient, *sends = refs[used + out : used + out + rows_of + 1]
            ordered, lined = rooms[2 * n], rooms[2 * n + 1]
            product_terms(block[...], hidden, [keep, *sends], part, both, width)
            for j in range(part):
                span = slice(j * width, (j + 1) * width)
                for i, ref in enumerate(hidden):
                    hi, mid, _ = place.block(0, i, 0) if over_mid else place.block(i, 0, 0)
                    for q in range(2):
                        core = 1 - place.core if q else place.core
                        at = pl.multiple_of(((mid if over_mid else hi) * 2 + core) * chans, chans)
                        ordered[pl.ds(at, chans), span] = ref[j, q * chans : (q + 1) * chans]
                for i, ref in enumerate(grad):
                    lined[i * both : (i + 1) * both, span] = ref[j]
            pairs = lax.dot_general(lined[...], ordered[...], (((1,), (1,)), ((), ())), preferred_element_type=F32)
            gradient[...] = pairs[:both]
            slices = pairs.shape[1] // width
            for i, send in enumerate(sends, 1):
                value = pairs[i * both : (i + 1) * both]
                high = value.astype(BF16)
                low = (value - high.astype(F32)).astype(BF16)
                for t in range(slices):
                    send[part + t] = high[:, t * width : (t + 1) * width]
                    send[part + slices + t] = low[:, t * width : (t + 1) * width]

    done = kernel_call(kernel, outs, args, scratch, after, HINTS["out"])
    return [
        (done[out], done[out + 1], done[out + 2 : out + 1 + rows_of]) for _, out, _, rows_of, _ in plans
    ]


def out_sums(first, second, filter_first, filter_second, count, after=()):
    part, both, width = first[0].shape
    chans, his, mids = both // 2, len(first), len(second)
    pair = filter_first.shape[1] // mids

    def kernel(*refs):
        terms = (refs[:his], refs[his : his + mids])
        own_rows, outs = refs[his + mids : his + mids + 2], refs[his + mids + 2 :]
        for n in range(2):

            @pl.loop(0, part)
            def _(i):
                total = terms[n][0][i].astype(F32)
                for term in terms[n][1:]:
                    total = total + term[i].astype(F32)
                outs[n][i] = total[:chans].astype(BF16)
                outs[2 + n][i] = total[chans:].astype(BF16)

        place = Place(count)

        def piece(n, back, columns):
            if back == 0:
                return own_rows[n][:, columns]
            slices = own_rows[n].shape[1] // width
            value = [
                terms[n][back][part + t].astype(F32) + terms[n][back][part + slices + t].astype(F32)
                for t in range(slices)
            ]
            return jnp.concatenate(value, axis=1)[:, columns]

        def chosen(n, at, mine, columns):
            value = piece(n, 0, columns)
            for back in range(1, len(terms[n])):
                value = jnp.where((mine + back) % len(terms[n]) == at, piece(n, back, columns), value)
            return value

        for hi in range(his):
            for mid in range(mids):
                block = chosen(0, hi, place.hi, slice(mid * pair, (mid + 1) * pair))
                block = block + chosen(1, mid, place.mid, slice(hi * pair, (hi + 1) * pair))
                at = (hi * mids + mid) * chans
                outs[4][at : at + chans] = block[:chans]
                outs[5][at : at + chans] = block[chans:]

    outs = [shaped((part, chans, width))] * 4 + [shaped((his * mids * chans, pair), F32)] * 2
    args = [*first, *second, filter_first, filter_second]
    done = kernel_call(kernel, outs, args, (), after, HINTS["out_sums"])
    return done[:2], done[2:4], done[4], done[5]


def slab_pieces(own, arrived, taps, slabs, after=()):
    rows = own.shape[0] // slabs
    wide = own.shape[1]

    def kernel(own, arrived, taps, *outs):
        slab = lax.axis_index("space")
        for apart, out in enumerate(outs):
            at = pl.ds(pl.multiple_of(jnp.bitwise_xor(slab, apart) * rows, rows), rows)
            out[:rows] = own[at] + arrived[at]
            out[rows:] = taps[...]

    piece = shaped((rows + taps.shape[0], wide), F32)
    return kernel_call(kernel, [piece] * slabs, [own, arrived, taps], (), after)


def last_outputs(own, arrived, pieces, count, planes, rows, scale, after=()):
    _, chans, width = own[0].shape
    lines, many = planes * rows, len(pieces)

    def kernel(*refs):
        raw, filter_out, tap_out, room, sems = refs[4 + many :]
        core = Place(count).core
        total = refs[4][...]
        for ref in refs[5 : 4 + many]:
            total = total + ref[...]
        total = total * scale
        filter_out[...] = total[:chans]
        tap_out[...] = total[chans : chans + 27, :chans]
        for mine in range(2):

            @pl.when(core == mine)
            def _():
                def load(line, group):
                    home, outer, at = line_home(line, rows)
                    return refs[outer if home == mine else 2 + outer][at, group]

                write_raw(load, raw, room, sems, chans, lines)

    outs = [
        shaped((chans * lines, width)),
        shaped((chans, pieces[0].shape[1]), F32),
        shaped((27, chans), F32),
    ]
    scratch = [pltpu.VMEM((chans * lines, width), BF16), pltpu.SemaphoreType.DMA((chans // 16,))]
    raw, filter_out, tap_out = kernel_call(
        kernel, outs, [*own, *arrived, *pieces], scratch, after, HINTS["last"], [ANYWHERE, IN_VMEM, IN_VMEM]
    )
    return raw.reshape(chans, planes, rows, width), filter_out, tap_out


def input_gradient(inner, outer, near, far, spread, count, planes, rows, after=()):
    _, _, chans, width = inner.shape
    half, lines = rows // 2, planes * rows

    def kernel(own, arrived, near, far, spread, raw, token, padded, cells, room, sems):
        core = Place(count).core
        token[...] = jnp.zeros(token.shape, F32)

        def line(p, r):
            home, at = r // half, r % half
            return jnp.where(core == home, own[at, p], arrived[at, p])

        fill_window(padded, line, *rims(near, far), planes, rows)

        def store(p, r, group, value):
            cells[p * rows + r, group] = value.astype(BF16)

        depthwise(padded, spread, planes, rows, list(range(rows)), store, True)
        write_raw(lambda line, group: cells[line, group], raw, room, sems, chans, lines)

    raw, token = kernel_call(
        kernel,
        [shaped((chans * lines, width)), shaped((8, width), F32)],
        [inner, outer, near, far, spread],
        [
            pltpu.VMEM(((planes + 2) * (rows + 2), chans, width), F32),
            pltpu.VMEM((lines, chans, width), BF16),
            pltpu.VMEM((chans * lines, width), BF16),
            pltpu.SemaphoreType.DMA((chans // 16,)),
        ],
        after,
        HINTS["input"],
        [ANYWHERE, IN_VMEM],
    )
    return raw.reshape(chans, planes, rows, width), token


def tap_sums(padded, back, before, count, planes, rows, others, wide, after=()):
    _, chans, width = padded.shape
    half, quarter = rows // 2, rows // 4
    last = before is not None
    args = [padded, *back] + ([before] if last else [])

    def kernel(padded, inner, outside, *refs):
        out, back = refs[-2 - last], refs[-1 - last]
        sums = refs[-1] if last else out
        core = Place(count).core
        home = 1 - core if others else core
        sums[...] = refs[0][...] if last else jnp.zeros(sums.shape, F32)
        lane = lax.broadcasted_iota(jnp.int32, (8, width), 1)
        deep = max(1, 4 // half)

        @pl.loop(0, planes)
        def _(p):
            for r in range(quarter):
                i = p * quarter + r
                back[r, p] = jnp.where(home == 0, outside[i].astype(F32), inner[i].astype(F32))
                back[quarter + r, p] = jnp.where(home == 0, inner[i].astype(F32), outside[i].astype(F32))

        @pl.loop(0, planes // deep)
        def _(i):
            for start in range(0, chans, 8):
                group = slice(start, start + 8)
                moved = {}
                for d in range(deep):
                    for r in range(half):
                        here = back[r, i * deep + d, group]
                        later = jnp.where(lane == width - 1, 0.0, pltpu.roll(here, width - 1, 1))
                        earlier = jnp.where(lane == 0, 0.0, pltpu.roll(here, 1, 1))
                        moved[d, r] = (later, here, earlier)
                for a in range(3):
                    images = {}
                    for d in range(deep):
                        base = (i * deep + d + a) * (rows + 2) + home * half
                        for line in range(half + 2):
                            images[d, line] = padded[base + line, group]
                    for b in range(3):
                        for e in range(3):
                            term = None
                            for (d, r), values in moved.items():
                                product = images[d, r + b] * values[e]
                                term = product if term is None else term + product
                            sums[9 * a + 3 * b + e, group] += term

        if last:
            row = lax.broadcasted_iota(jnp.int32, (chans, wide), 0)
            col = lax.broadcasted_iota(jnp.int32, (chans, wide), 1)
            for tap in range(27):
                total = jnp.sum(sums[tap], axis=1, keepdims=True)
                out[tap : tap + 1] = jnp.sum(jnp.where(row == col, total, 0.0), axis=0, keepdims=True)
            out[27:] = jnp.zeros((5, wide), F32)

    running = (27, chans, width)
    scratch = [pltpu.VMEM(running, F32)] if last else []
    outs = [shaped((32, wide) if last else running, F32), shaped((half, planes, chans, width), F32)]
    return kernel_call(kernel, outs, args, scratch, after, HINTS["late_taps" if last else "taps"])


def body(images, depth_filter, point_filter, grad_out):
    chans, planes, rows, width = images.shape
    count, slabs = lax.axis_size("chan"), lax.axis_size("space")
    his, mids = count // 4, 2
    place = Place(count)
    grad_scale = 1.0 / math.sqrt(planes * rows * width * slabs)

    def moved(value, target):
        pairs = []
        for i in range(count):
            hi, mid, core = target(i // 2 // mids, i // 2 % mids, i % 2)
            pairs.append((i, (hi % his * mids + mid % mids) * 2 + core))
        return lax.ppermute(value, "chan", pairs)

    def to_core(value):
        return moved(value, lambda hi, mid, core: (hi, mid, 1 - core))

    def along_hi(value, by):
        return moved(value, lambda hi, mid, core: (hi + by, mid, core))

    def along_mid(value, by):
        return moved(value, lambda hi, mid, core: (hi, mid + by, core))

    def halo(near, far):
        swaps = [[(i + d, i + 1 - d) for i in range(first, slabs - 1, 2) for d in range(2)] for first in range(2)]
        return lax.ppermute(near, "space", swaps[0]), lax.ppermute(far, "space", swaps[1])

    def exchanged(value, apart):
        return lax.ppermute(value, "space", [(i, i ^ apart) for i in range(slabs)])

    filter_arrived = to_core(point_filter)
    grad_own, grad_other = relayout_grad(grad_out, count)
    grad_arrived = to_core(grad_other)
    cells, near, far = relayout_images(images, [grad_own, filter_arrived])
    image_rims = halo(near, far)
    to_hi, to_mid, filter_hi, filter_mid = pack_grad(
        grad_own, grad_arrived, point_filter, filter_arrived, count, [cells]
    )
    grads_hi = [along_hi(value, s) for s, value in enumerate(to_hi, 1)]
    grads_mid = [along_mid(value, t) for t, value in enumerate(to_mid, 1)]

    windows = (cells, *image_rims)
    plan = (count, planes, rows)
    inner_own, inner_other, spread = hidden_part(*windows, depth_filter, *plan, False, [to_hi[0]])
    inner_arrived = to_core(inner_other)
    outer_own, outer_other, padded = hidden_part(*windows, spread, *plan, True, [inner_own])
    outer_arrived = to_core(outer_other)
    hidden_first, hidden_second = joined([inner_own, outer_own], [inner_arrived, outer_arrived])
    hiddens_mid = [hidden_first] + [along_mid(hidden_first, t) for t in range(1, mids)]
    hiddens_hi = [hidden_second] + [along_hi(hidden_second, s) for s in range(1, his)]

    (keep_first, send_first, block_first), (keep_second, send_second, block_second) = back_terms(
        [(to_hi[0], grads_hi, filter_hi, mids - 1), (to_mid[0], grads_mid, filter_mid, his - 1)], [hidden_first]
    )
    back_first = [keep_first] + [along_mid(value, -t) for t, value in enumerate(send_first, 1)]
    back_second = [keep_second] + [along_hi(value, -s) for s, value in enumerate(send_second, 1)]

    (out_first, pg_first, send_first), (out_second, pg_second, send_second) = out_terms(
        [
            (block_first, hiddens_mid, [to_hi[0], *grads_hi], True),
            (block_second, hiddens_hi, [to_mid[0], *grads_mid], False),
        ],
        count,
        [keep_first],
    )
    latest = out_first
    out_first = [out_first] + [along_hi(value, -s) for s, value in enumerate(send_first, 1)]
    out_second = [out_second] + [along_mid(value, -t) for t, value in enumerate(send_second, 1)]

    back_own, back_other = summed_parts(back_first, back_second, [latest])
    back_arrived = [to_core(value) for value in back_other]
    wide = his * mids * 2 * chans // slabs
    taps, back_own_lines = tap_sums(padded, back_own, None, *plan, False, wide)
    edges = edge_rows(back_own[1], back_arrived[1], count, rows, [taps])
    back_rims = halo(*edges)
    taps, back_arrived_lines = tap_sums(padded, back_arrived, taps, *plan, True, wide, [edges[0]])
    out_own, out_other, own, other = out_sums(out_first, out_second, pg_first, pg_second, count, [taps])
    out_arrived = [to_core(value) for value in out_other]
    chip_arrived = to_core(other)
    if own.shape[1] != wide:

        def by_slab(value):
            value = value.reshape(his * mids, chans, -1).swapaxes(0, 1).reshape(chans, slabs, wide)
            return value.swapaxes(0, 1).reshape(-1, wide)

        own, chip_arrived = by_slab(own), by_slab(chip_arrived)
    pieces = slab_pieces(own, chip_arrived, taps, slabs)
    input_grad, latest = input_gradient(back_own_lines, back_arrived_lines, *back_rims, spread, *plan, [pieces[0]])
    pieces = [pieces[0]] + [exchanged(piece, apart) for apart, piece in enumerate(pieces[1:], 1)]
    block_out, point_grad, depth_grad = last_outputs(out_own, out_arrived, pieces, *plan, grad_scale, [latest])
    return block_out, point_grad, input_grad, depth_grad


def solution(mesh):
    placed = (
        P("chan", None, "space", None),
        P(None, "chan"),
        P("chan", None),
        P("chan", None, "space", None),
    )
    return jax.shard_map(
        body,
        mesh=mesh,
        in_specs=placed,
        out_specs=(
            P("chan", None, "space", None),
            P("chan", "space"),
            P("chan", None, "space", None),
            P(None, "chan"),
        ),
        check_vma=False,
    )
```

```python
import math

import jax
import jax.numpy as jnp
from jax import lax
from jax.experimental import pallas as pl
from jax.experimental.pallas import tpu as pltpu
from jax.sharding import PartitionSpec as P

F32, BF16 = jnp.float32, jnp.bfloat16
HINTS = dict(
    inner=0.1, outer=0.1, back=0.1, out=0.1, sums=0.1, out_sums=0.1, taps=0.1, late_taps=0.1, input=20, pack=0.1, last=0.1, relayout=1.5
)
RATE = 10**9
IN_VMEM = pl.BlockSpec(memory_space=pltpu.VMEM)
ANYWHERE = pl.BlockSpec(memory_space=pl.ANY)


class Place:
    def __init__(self, count):
        self.mids = 2
        self.his = count // 4
        index = lax.axis_index("chan")
        self.core = index % 2
        self.mid = index // 2 % self.mids
        self.hi = index // 2 // self.mids

    def block(self, hi_back, mid_back, core_flip):
        hi = (self.hi + self.his - hi_back) % self.his
        mid = (self.mid + self.mids - mid_back) % self.mids
        core = 1 - self.core if core_flip else self.core
        return hi, mid, core

    def flat(self, hi, mid, core):
        return (hi * self.mids + mid) * 2 + core


def size_of(shape, dtype):
    return math.prod(shape) * jnp.dtype(dtype).itemsize


def rims(near, far):
    odd = lax.axis_index("space") % 2 == 1

    def up(p):
        return jnp.where(odd, near[p].astype(F32), far[p].astype(F32))

    def down(p):
        return jnp.where(odd, far[p].astype(F32), near[p].astype(F32))

    return up, down


def kernel_call(kernel, outs, args, scratch=(), after=(), micros=0.1, places=None):
    used = len(args)

    def run(*refs):
        kernel(*refs[:used], *refs[used + len(after) :])

    held = [x for x in (*args, *outs, *scratch) if jnp.issubdtype(x.dtype, jnp.floating)]
    room = sum(size_of(x.shape, x.dtype) for x in held)
    return pl.pallas_call(
        run,
        out_shape=outs,
        in_specs=[IN_VMEM] * used + [ANYWHERE] * len(after),
        out_specs=places or [IN_VMEM] * len(outs),
        scratch_shapes=list(scratch),
        compiler_params=pltpu.CompilerParams(vmem_limit_bytes=room + 4 * 2**20),
        cost_estimate=pl.CostEstimate(flops=int(micros * RATE), bytes_accessed=0, transcendentals=0),
    )(*args, *after)


def shaped(shape, dtype=BF16):
    return jax.ShapeDtypeStruct(shape, dtype)


def line_home(line, rows):
    plane, row = divmod(line, rows)
    quarter = rows // 4
    core = row // (2 * quarter)
    outer = (row // quarter) in (0, 3)
    return core, outer, plane * quarter + row % quarter


def raw_to_cells(raw, chans, store):
    lines = raw.shape[0] // chans

    @pl.loop(0, chans // 16)
    def _(g):
        group = pl.ds(pl.multiple_of(g * 16, 16), 16)
        for first in range(0, lines, 16):
            block = [raw[pl.ds(pl.multiple_of((g * 16 + c) * lines + first, 16), 16), :] for c in range(16)]
            turned = jnp.swapaxes(jnp.stack([b.astype(F32) for b in block]), 0, 1).astype(BF16)
            for i in range(16):
                store(first + i, group, turned[i])


def write_raw(load, raw, room, sems, chans, lines):
    def copy(start):
        rows = slice(start * lines, (start + 16) * lines)
        return pltpu.make_async_copy(room.at[rows], raw.at[rows], sems.at[start // 16])

    for start in range(0, chans, 16):
        group = slice(start, start + 16)
        for first in range(0, lines, 16):
            block = jnp.stack([load(first + i, group).astype(F32) for i in range(16)])
            turned = jnp.swapaxes(block, 0, 1).astype(BF16)
            for c in range(16):
                at = (start + c) * lines + first
                room[at : at + 16] = turned[c]
        copy(start).start()
    for start in range(0, chans, 16):
        copy(start).wait()


def relayout_images(images, after=()):
    chans, planes, rows, width = images.shape

    def kernel(raw, cells, near, far):
        odd = lax.axis_index("space") % 2 == 1

        def store(line, group, value):
            cells[line, group] = value

        raw_to_cells(raw, chans, store)
        for parity, (first, last) in enumerate(((far, near), (near, far))):

            @pl.when(odd == bool(parity))
            def _():
                @pl.loop(0, planes)
                def _(p):
                    first[p] = cells[p * rows]
                    last[p] = cells[p * rows + rows - 1]

    edge = shaped((planes, chans, width))
    return kernel_call(
        kernel,
        [shaped((planes * rows, chans, width)), edge, edge],
        [images.reshape(-1, width)],
        (),
        after,
        HINTS["relayout"],
    )


def relayout_grad(grad_out, count, after=()):
    chans, planes, rows, width = grad_out.shape
    half = planes * rows // 2

    def kernel(raw, own, other):
        core = Place(count).core
        for mine in range(2):

            @pl.when(core == mine)
            def _():
                def store(line, group, value):
                    home, outer, at = line_home(line, rows)
                    out = own if home == mine else other
                    out[outer * (half // 2) + at, group] = value

                raw_to_cells(raw, chans, store)

    part = shaped((half, chans, width))
    return kernel_call(kernel, [part, part], [grad_out.reshape(-1, width)], (), after, HINTS["relayout"])


def tap_planes(weights, spread, chans, width):
    turned = jnp.concatenate([weights, jnp.zeros((5, chans), F32)], axis=0).T
    for k in range(27):
        spread[k] = jnp.broadcast_to(turned[:, k : k + 1], (chans, width))


def fill_window(padded, line, up, down, planes, rows):
    zero = jnp.zeros(padded.shape[1:], F32)
    for n in range(rows + 2):
        padded[n] = zero
        padded[(planes + 1) * (rows + 2) + n] = zero

    @pl.loop(0, planes)
    def _(p):
        base = (p + 1) * (rows + 2)
        if up is not None:
            padded[base] = up(p)
            padded[base + rows + 1] = down(p)
        for r in range(rows):
            padded[base + 1 + r] = line(p, r).astype(F32)


def depthwise(padded, spread, planes, rows, wanted, store, flipped):
    _, chans, width = padded.shape
    lane = lax.broadcasted_iota(jnp.int32, (8, width), 1)
    deep = 4 // len(wanted)

    def summed(first, group):
        sums = {(d, r): [None] * 3 for d in range(deep) for r in wanted}
        for a in range(3):
            taps = [[spread[26 - 9 * a - 3 * b - e if flipped else 9 * a + 3 * b + e, group] for e in range(3)] for b in range(3)]
            for d in range(deep):
                for line in sorted({r + b for r in wanted for b in range(3)}):
                    cells = padded[(first + d + a) * (rows + 2) + line, group]
                    for b in range(3):
                        if line - b in wanted:
                            held = sums[d, line - b]
                            for e in range(3):
                                term = taps[b][e] * cells
                                held[e] = term if held[e] is None else held[e] + term
        for place, held in sums.items():
            before = jnp.where(lane == 0, 0.0, pltpu.roll(held[0], 1, 1))
            after = jnp.where(lane == width - 1, 0.0, pltpu.roll(held[2], width - 1, 1))
            sums[place] = held[1] + before + after
        return sums

    @pl.loop(0, planes // deep)
    def _(i):
        for start in range(0, chans, 16):
            low = summed(i * deep, slice(start, start + 8))
            high = summed(i * deep, slice(start + 8, start + 16))
            for d, r in low:
                both = jnp.concatenate([low[d, r], high[d, r]], axis=0)
                store(i * deep + d, r, slice(start, start + 16), both)


def hidden_part(cells, near, far, weights, count, planes, rows, outer, after=()):
    _, chans, width = cells.shape
    quarter = rows // 4
    args = [cells, near, far, weights] if outer else [cells, weights]
    wanted = [r for r in range(rows) if ((r // quarter) in (0, 3)) == outer]

    def kernel(*refs):
        cells = refs[0]
        own, other, extra, both = refs[len(args) : len(args) + 4]
        core = Place(count).core
        if outer:
            padded, spread = extra, refs[3]
            up, down = rims(*refs[1:3])
        else:
            padded, spread = refs[-1], extra
            up, down = None, None
            tap_planes(refs[1][...], spread, chans, width)
        fill_window(padded, lambda p, r: cells[p * rows + r], up, down, planes, rows)

        def put(p, r, group, value):
            home, _, at = line_home(r, rows)
            both[home, p * quarter + at, group] = value.astype(BF16)

        depthwise(padded, spread, planes, rows, wanted, put, False)

        @pl.loop(0, planes * quarter)
        def _(i):
            own[i] = both[core, i]
            other[i] = both[1 - core, i]

    part = shaped((planes * quarter, chans, width))
    window = ((planes + 2) * (rows + 2), chans, width)
    outs = [part, part, shaped(window if outer else (27, chans, width), F32)]
    scratch = [pltpu.VMEM((2, planes * quarter, chans, width), BF16)]
    if not outer:
        scratch.append(pltpu.VMEM(window, F32))
    return kernel_call(kernel, outs, args, scratch, after, HINTS["outer" if outer else "inner"])


def picked(table, starts, chans):
    total, wide = table.shape[1], len(starts) * chans
    col = lax.broadcasted_iota(jnp.int32, (total, wide), 1)
    row = lax.broadcasted_iota(jnp.int32, (total, wide), 0)
    want = jnp.zeros((total, wide), jnp.int32)
    for b, start in enumerate(starts):
        want = jnp.where((col >= b * chans) & (col < (b + 1) * chans), start + col - b * chans, want)
    choice = jnp.where(row == want, 1.0, 0.0).astype(BF16)
    return jnp.dot(table, choice, preferred_element_type=F32).astype(BF16)


def pack_grad(own, arrived, filter_own, filter_arrived, count, after=()):
    half, chans, width = own.shape
    part = half // 2
    his, mids = count // 4, 2
    hi_slices, mid_slices = mids * 2 * chans // width, his * 2 * chans // width

    def kernel(own, arrived, filter_own, filter_arrived, *outs):
        place = Place(count)
        table = jnp.concatenate([filter_own[...], filter_arrived[...]], axis=0)
        to_hi, to_mid = outs[: his - 1], outs[his - 1 : his + mids - 2]
        mine_hi, mine_mid = outs[-2:]

        def columns(for_hi, hi, mid):
            if for_hi:
                cells = [(hi, (mid + mids - t) % mids) for t in range(mids)]
            else:
                cells = [((hi + his - s) % his, mid) for s in range(his)]
            starts = [
                place.flat(hi_, mid_, place.core if q == 0 else 1 - place.core) * chans
                for hi_, mid_ in cells
                for q in range(2)
            ]
            return picked(table, starts, chans)

        def put(out, base, value):
            for i in range(value.shape[1] // width):
                out[base + i] = value[:, i * width : (i + 1) * width]

        for refs, offset in ((to_hi, 0), (to_mid, part)):

            @pl.loop(0, part)
            def _(i):
                for ref in refs:
                    ref[i, :chans] = own[offset + i]
                    ref[i, chans:] = arrived[offset + i]

        for s, ref in enumerate(to_hi, 1):
            put(ref, part, columns(True, (place.hi + s) % his, place.mid))
        for t, ref in enumerate(to_mid, 1):
            put(ref, part, columns(False, place.hi, (place.mid + t) % mids))
        put(mine_hi, 0, columns(True, place.hi, place.mid))
        put(mine_mid, 0, columns(False, place.hi, place.mid))

    outs = (
        [shaped((part + hi_slices, 2 * chans, width))] * (his - 1)
        + [shaped((part + mid_slices, 2 * chans, width))] * (mids - 1)
        + [shaped((hi_slices, 2 * chans, width)), shaped((mid_slices, 2 * chans, width))]
    )
    outs = kernel_call(kernel, outs, [own, arrived, filter_own, filter_arrived], (), after, micros=HINTS["pack"])
    return outs[: his - 1], outs[his - 1 : his + mids - 2], outs[-2], outs[-1]


def product_terms(weights, blocks, outs, part, both, width):
    step = math.gcd(part, 4)

    @pl.loop(0, part // step)
    def _(i):
        cells = jnp.concatenate(
            [jnp.concatenate([ref[i * step + j] for ref in blocks], axis=0) for j in range(step)], axis=1
        )
        product = jnp.dot(weights, cells, preferred_element_type=F32)
        for n, out in enumerate(outs):
            for j in range(step):
                term = product[n * both : (n + 1) * both, j * width : (j + 1) * width]
                out[i * step + j] = term.astype(out.dtype)


def back_terms(parts, after=()):
    args, outs, plans = [], [], []
    for mine, arrived, filter_mine, sends in parts:
        slices, both, width = filter_mine.shape
        part = mine.shape[0] - slices
        plans.append((len(args), len(outs), len(arrived), sends, slices, part))
        args += [mine, filter_mine, *arrived]
        outs += [shaped((part, both, width), F32)] + [shaped((part, both, width))] * sends + [shaped(((1 + len(arrived)) * both, slices * width))]
    used = len(args)

    def kernel(*refs):
        for start, out, many, sends, slices, part in plans:
            mine, filter_mine, *arrived = refs[start : start + 2 + many]
            rows = [jnp.concatenate([filter_mine[i] for i in range(slices)], axis=1)]
            for ref in arrived:
                rows.append(jnp.concatenate([ref[part + i] for i in range(slices)], axis=1))
            block = jnp.concatenate(rows, axis=0)
            refs[used + out + sends + 1][...] = block
            turned = block.astype(F32).T.astype(BF16)
            product_terms(turned, [mine, *arrived], refs[used + out : used + out + sends + 1], part, both, width)

    done = kernel_call(kernel, outs, args, (), after, micros=HINTS["back"])
    return [(done[o], done[o + 1 : o + 1 + sends], done[o + 1 + sends]) for _, o, _, sends, _, _ in plans]


def summed_parts(first, second, after=()):
    part, both, width = first[0].shape
    chans = both // 2

    def kernel(*refs):
        outs = refs[-4:]
        for n, terms in enumerate((refs[: len(first)], refs[len(first) : -4])):

            @pl.loop(0, part)
            def _(i):
                total = terms[0][i].astype(F32)
                for term in terms[1:]:
                    total = total + term[i].astype(F32)
                outs[n][i] = total[:chans].astype(BF16)
                outs[2 + n][i] = total[chans:].astype(BF16)

    done = kernel_call(kernel, [shaped((part, chans, width))] * 4, [*first, *second], (), after, HINTS["sums"])
    return done[:2], done[2:]


def edge_rows(own, arrived, count, rows, after=()):
    part, chans, width = own.shape
    quarter = rows // 4
    planes = part // quarter

    def kernel(own, arrived, near, far):
        core = Place(count).core
        odd = lax.axis_index("space") % 2
        for mine in range(2):
            for parity in range(2):

                @pl.when((core == mine) & (odd == parity))
                def _():
                    first, last = (own, arrived) if mine == 0 else (arrived, own)
                    to_first, to_last = (near, far) if parity else (far, near)

                    @pl.loop(0, planes)
                    def _(p):
                        to_first[p] = first[p * quarter]
                        to_last[p] = last[p * quarter + quarter - 1]

    edge = shaped((planes, chans, width))
    return kernel_call(kernel, [edge, edge], [own, arrived], (), after)


def joined(own, arrived, after=()):
    part, chans, width = own[0].shape
    many = len(own)

    def kernel(*refs):
        @pl.loop(0, part)
        def _(i):
            for a, b, out in zip(refs[:many], refs[many : 2 * many], refs[2 * many :]):
                out[i, :chans] = a[i]
                out[i, chans:] = b[i]

    return kernel_call(kernel, [shaped((part, 2 * chans, width))] * many, [*own, *arrived], (), after)


def out_terms(parts, count, after=()):
    args, plans, outs, scratch = [], [], [], []
    for block, hiddens, grads, over_mid in parts:
        part, both, width = hiddens[0].shape
        chans, wide = both // 2, len(hiddens) * both
        plans.append((len(args), len(outs), len(hiddens), len(grads), over_mid))
        args += [block, *hiddens, *grads]
        outs += [shaped((part, both, width), F32), shaped((both, wide), F32)]
        outs += [shaped((part + 2 * wide // width, both, width))] * (len(grads) - 1)
        scratch += [pltpu.VMEM((wide, part * width), BF16), pltpu.VMEM((len(grads) * both, part * width), BF16)]
    used = len(args)

    def kernel(*refs):
        place = Place(count)
        rooms = refs[used + len(outs) :]
        for n, (start, out, cols_of, rows_of, over_mid) in enumerate(plans):
            block, hidden = refs[start], refs[start + 1 : start + 1 + cols_of]
            grad = refs[start + 1 + cols_of : start + 1 + cols_of + rows_of]
            keep, gradient, *sends = refs[used + out : used + out + rows_of + 1]
            ordered, lined = rooms[2 * n], rooms[2 * n + 1]
            product_terms(block[...], hidden, [keep, *sends], part, both, width)
            for j in range(part):
                span = slice(j * width, (j + 1) * width)
                for i, ref in enumerate(hidden):
                    hi, mid, _ = place.block(0, i, 0) if over_mid else place.block(i, 0, 0)
                    for q in range(2):
                        core = 1 - place.core if q else place.core
                        at = pl.multiple_of(((mid if over_mid else hi) * 2 + core) * chans, chans)
                        ordered[pl.ds(at, chans), span] = ref[j, q * chans : (q + 1) * chans]
                for i, ref in enumerate(grad):
                    lined[i * both : (i + 1) * both, span] = ref[j]
            pairs = lax.dot_general(lined[...], ordered[...], (((1,), (1,)), ((), ())), preferred_element_type=F32)
            gradient[...] = pairs[:both]
            slices = pairs.shape[1] // width
            for i, send in enumerate(sends, 1):
                value = pairs[i * both : (i + 1) * both]
                high = value.astype(BF16)
                low = (value - high.astype(F32)).astype(BF16)
                for t in range(slices):
                    send[part + t] = high[:, t * width : (t + 1) * width]
                    send[part + slices + t] = low[:, t * width : (t + 1) * width]

    done = kernel_call(kernel, outs, args, scratch, after, HINTS["out"])
    return [
        (done[out], done[out + 1], done[out + 2 : out + 1 + rows_of]) for _, out, _, rows_of, _ in plans
    ]


def out_sums(first, second, filter_first, filter_second, count, after=()):
    part, both, width = first[0].shape
    chans, his, mids = both // 2, len(first), len(second)
    pair = filter_first.shape[1] // mids

    def kernel(*refs):
        terms = (refs[:his], refs[his : his + mids])
        own_rows, outs = refs[his + mids : his + mids + 2], refs[his + mids + 2 :]
        for n in range(2):

            @pl.loop(0, part)
            def _(i):
                total = terms[n][0][i].astype(F32)
                for term in terms[n][1:]:
                    total = total + term[i].astype(F32)
                outs[n][i] = total[:chans].astype(BF16)
                outs[2 + n][i] = total[chans:].astype(BF16)

        place = Place(count)

        def piece(n, back, columns):
            if back == 0:
                return own_rows[n][:, columns]
            slices = own_rows[n].shape[1] // width
            value = [
                terms[n][back][part + t].astype(F32) + terms[n][back][part + slices + t].astype(F32)
                for t in range(slices)
            ]
            return jnp.concatenate(value, axis=1)[:, columns]

        def chosen(n, at, mine, columns):
            value = piece(n, 0, columns)
            for back in range(1, len(terms[n])):
                value = jnp.where((mine + back) % len(terms[n]) == at, piece(n, back, columns), value)
            return value

        for hi in range(his):
            for mid in range(mids):
                block = chosen(0, hi, place.hi, slice(mid * pair, (mid + 1) * pair))
                block = block + chosen(1, mid, place.mid, slice(hi * pair, (hi + 1) * pair))
                at = (hi * mids + mid) * chans
                outs[4][at : at + chans] = block[:chans]
                outs[5][at : at + chans] = block[chans:]

    outs = [shaped((part, chans, width))] * 4 + [shaped((his * mids * chans, pair), F32)] * 2
    args = [*first, *second, filter_first, filter_second]
    done = kernel_call(kernel, outs, args, (), after, HINTS["out_sums"])
    return done[:2], done[2:4], done[4], done[5]


def slab_pieces(own, arrived, taps, slabs, after=()):
    rows = own.shape[0] // slabs
    wide = own.shape[1]

    def kernel(own, arrived, taps, *outs):
        slab = lax.axis_index("space")
        for apart, out in enumerate(outs):
            at = pl.ds(pl.multiple_of(jnp.bitwise_xor(slab, apart) * rows, rows), rows)
            out[:rows] = own[at] + arrived[at]
            out[rows:] = taps[...]

    piece = shaped((rows + taps.shape[0], wide), F32)
    return kernel_call(kernel, [piece] * slabs, [own, arrived, taps], (), after)


def last_outputs(own, arrived, pieces, count, planes, rows, scale, after=()):
    _, chans, width = own[0].shape
    lines, many = planes * rows, len(pieces)

    def kernel(*refs):
        raw, filter_out, tap_out, room, sems = refs[4 + many :]
        core = Place(count).core
        total = refs[4][...]
        for ref in refs[5 : 4 + many]:
            total = total + ref[...]
        total = total * scale
        filter_out[...] = total[:chans]
        tap_out[...] = total[chans : chans + 27, :chans]
        for mine in range(2):

            @pl.when(core == mine)
            def _():
                def load(line, group):
                    home, outer, at = line_home(line, rows)
                    return refs[outer if home == mine else 2 + outer][at, group]

                write_raw(load, raw, room, sems, chans, lines)

    outs = [
        shaped((chans * lines, width)),
        shaped((chans, pieces[0].shape[1]), F32),
        shaped((27, chans), F32),
    ]
    scratch = [pltpu.VMEM((chans * lines, width), BF16), pltpu.SemaphoreType.DMA((chans // 16,))]
    raw, filter_out, tap_out = kernel_call(
        kernel, outs, [*own, *arrived, *pieces], scratch, after, HINTS["last"], [ANYWHERE, IN_VMEM, IN_VMEM]
    )
    return raw.reshape(chans, planes, rows, width), filter_out, tap_out


def input_gradient(inner, outer, near, far, spread, count, planes, rows, after=()):
    _, _, chans, width = inner.shape
    half, lines = rows // 2, planes * rows

    def kernel(own, arrived, near, far, spread, raw, token, padded, cells, room, sems):
        core = Place(count).core
        token[...] = jnp.zeros(token.shape, F32)

        def line(p, r):
            home, at = r // half, r % half
            return jnp.where(core == home, own[at, p], arrived[at, p])

        fill_window(padded, line, *rims(near, far), planes, rows)

        def store(p, r, group, value):
            cells[p * rows + r, group] = value.astype(BF16)

        depthwise(padded, spread, planes, rows, list(range(rows)), store, True)
        write_raw(lambda line, group: cells[line, group], raw, room, sems, chans, lines)

    raw, token = kernel_call(
        kernel,
        [shaped((chans * lines, width)), shaped((8, width), F32)],
        [inner, outer, near, far, spread],
        [
            pltpu.VMEM(((planes + 2) * (rows + 2), chans, width), F32),
            pltpu.VMEM((lines, chans, width), BF16),
            pltpu.VMEM((chans * lines, width), BF16),
            pltpu.SemaphoreType.DMA((chans // 16,)),
        ],
        after,
        HINTS["input"],
        [ANYWHERE, IN_VMEM],
    )
    return raw.reshape(chans, planes, rows, width), token


def tap_sums(padded, back, before, count, planes, rows, others, wide, after=()):
    _, chans, width = padded.shape
    half, quarter = rows // 2, rows // 4
    last = before is not None
    args = [padded, *back] + ([before] if last else [])

    def kernel(padded, inner, outside, *refs):
        out, back = refs[-2 - last], refs[-1 - last]
        sums = refs[-1] if last else out
        core = Place(count).core
        home = 1 - core if others else core
        sums[...] = refs[0][...] if last else jnp.zeros(sums.shape, F32)
        lane = lax.broadcasted_iota(jnp.int32, (8, width), 1)
        deep = max(1, 4 // half)

        @pl.loop(0, planes)
        def _(p):
            for r in range(quarter):
                i = p * quarter + r
                back[r, p] = jnp.where(home == 0, outside[i].astype(F32), inner[i].astype(F32))
                back[quarter + r, p] = jnp.where(home == 0, inner[i].astype(F32), outside[i].astype(F32))

        @pl.loop(0, planes // deep)
        def _(i):
            for start in range(0, chans, 8):
                group = slice(start, start + 8)
                moved = {}
                for d in range(deep):
                    for r in range(half):
                        here = back[r, i * deep + d, group]
                        later = jnp.where(lane == width - 1, 0.0, pltpu.roll(here, width - 1, 1))
                        earlier = jnp.where(lane == 0, 0.0, pltpu.roll(here, 1, 1))
                        moved[d, r] = (later, here, earlier)
                for a in range(3):
                    images = {}
                    for d in range(deep):
                        base = (i * deep + d + a) * (rows + 2) + home * half
                        for line in range(half + 2):
                            images[d, line] = padded[base + line, group]
                    for b in range(3):
                        for e in range(3):
                            term = None
                            for (d, r), values in moved.items():
                                product = images[d, r + b] * values[e]
                                term = product if term is None else term + product
                            sums[9 * a + 3 * b + e, group] += term

        if last:
            row = lax.broadcasted_iota(jnp.int32, (chans, wide), 0)
            col = lax.broadcasted_iota(jnp.int32, (chans, wide), 1)
            for tap in range(27):
                total = jnp.sum(sums[tap], axis=1, keepdims=True)
                out[tap : tap + 1] = jnp.sum(jnp.where(row == col, total, 0.0), axis=0, keepdims=True)
            out[27:] = jnp.zeros((5, wide), F32)

    running = (27, chans, width)
    scratch = [pltpu.VMEM(running, F32)] if last else []
    outs = [shaped((32, wide) if last else running, F32), shaped((half, planes, chans, width), F32)]
    return kernel_call(kernel, outs, args, scratch, after, HINTS["late_taps" if last else "taps"])


def body(images, depth_filter, point_filter, grad_out):
    chans, planes, rows, width = images.shape
    count, slabs = lax.axis_size("chan"), lax.axis_size("space")
    his, mids = count // 4, 2
    place = Place(count)
    grad_scale = 1.0 / math.sqrt(planes * rows * width * slabs)

    def moved(value, target):
        pairs = []
        for i in range(count):
            hi, mid, core = target(i // 2 // mids, i // 2 % mids, i % 2)
            pairs.append((i, (hi % his * mids + mid % mids) * 2 + core))
        return lax.ppermute(value, "chan", pairs)

    def to_core(value):
        return moved(value, lambda hi, mid, core: (hi, mid, 1 - core))

    def along_hi(value, by):
        return moved(value, lambda hi, mid, core: (hi + by, mid, core))

    def along_mid(value, by):
        return moved(value, lambda hi, mid, core: (hi, mid + by, core))

    def halo(near, far):
        swaps = [[(i + d, i + 1 - d) for i in range(first, slabs - 1, 2) for d in range(2)] for first in range(2)]
        return lax.ppermute(near, "space", swaps[0]), lax.ppermute(far, "space", swaps[1])

    def exchanged(value, apart):
        return lax.ppermute(value, "space", [(i, i ^ apart) for i in range(slabs)])

    filter_arrived = to_core(point_filter)
    grad_own, grad_other = relayout_grad(grad_out, count, [filter_arrived])
    grad_arrived = to_core(grad_other)
    cells, near, far = relayout_images(images, [grad_own])
    image_rims = halo(near, far)
    to_hi, to_mid, filter_hi, filter_mid = pack_grad(
        grad_own, grad_arrived, point_filter, filter_arrived, count, [cells]
    )
    grads_hi = [along_hi(value, s) for s, value in enumerate(to_hi, 1)]
    grads_mid = [along_mid(value, t) for t, value in enumerate(to_mid, 1)]

    windows = (cells, *image_rims)
    plan = (count, planes, rows)
    inner_own, inner_other, spread = hidden_part(*windows, depth_filter, *plan, False, [to_hi[0]])
    inner_arrived = to_core(inner_other)
    outer_own, outer_other, padded = hidden_part(*windows, spread, *plan, True, [inner_own])
    outer_arrived = to_core(outer_other)
    hidden_first, hidden_second = joined([inner_own, outer_own], [inner_arrived, outer_arrived])
    hiddens_mid = [hidden_first] + [along_mid(hidden_first, t) for t in range(1, mids)]
    hiddens_hi = [hidden_second] + [along_hi(hidden_second, s) for s in range(1, his)]

    (keep_first, send_first, block_first), (keep_second, send_second, block_second) = back_terms(
        [(to_hi[0], grads_hi, filter_hi, mids - 1), (to_mid[0], grads_mid, filter_mid, his - 1)], [hidden_first]
    )
    back_first = [keep_first] + [along_mid(value, -t) for t, value in enumerate(send_first, 1)]
    back_second = [keep_second] + [along_hi(value, -s) for s, value in enumerate(send_second, 1)]

    (out_first, pg_first, send_first), (out_second, pg_second, send_second) = out_terms(
        [
            (block_first, hiddens_mid, [to_hi[0], *grads_hi], True),
            (block_second, hiddens_hi, [to_mid[0], *grads_mid], False),
        ],
        count,
        [keep_first],
    )
    latest = out_first
    out_first = [out_first] + [along_hi(value, -s) for s, value in enumerate(send_first, 1)]
    out_second = [out_second] + [along_mid(value, -t) for t, value in enumerate(send_second, 1)]

    back_own, back_other = summed_parts(back_first, back_second, [latest])
    back_arrived = [to_core(value) for value in back_other]
    wide = his * mids * 2 * chans // slabs
    taps, back_own_lines = tap_sums(padded, back_own, None, *plan, False, wide)
    edges = edge_rows(back_own[1], back_arrived[1], count, rows, [taps])
    back_rims = halo(*edges)
    taps, back_arrived_lines = tap_sums(padded, back_arrived, taps, *plan, True, wide, [edges[0]])
    out_own, out_other, own, other = out_sums(out_first, out_second, pg_first, pg_second, count, [taps])
    out_arrived = [to_core(value) for value in out_other]
    chip_arrived = to_core(other)
    if own.shape[1] != wide:

        def by_slab(value):
            value = value.reshape(his * mids, chans, -1).swapaxes(0, 1).reshape(chans, slabs, wide)
            return value.swapaxes(0, 1).reshape(-1, wide)

        own, chip_arrived = by_slab(own), by_slab(chip_arrived)
    pieces = slab_pieces(own, chip_arrived, taps, slabs)
    input_grad, latest = input_gradient(back_own_lines, back_arrived_lines, *back_rims, spread, *plan, [pieces[0]])
    pieces = [pieces[0]] + [exchanged(piece, apart) for apart, piece in enumerate(pieces[1:], 1)]
    block_out, point_grad, depth_grad = last_outputs(out_own, out_arrived, pieces, *plan, grad_scale, [latest])
    return block_out, point_grad, input_grad, depth_grad


def solution(mesh):
    placed = (
        P("chan", None, "space", None),
        P(None, "chan"),
        P("chan", None),
        P("chan", None, "space", None),
    )
    return jax.shard_map(
        body,
        mesh=mesh,
        in_specs=placed,
        out_specs=(
            P("chan", None, "space", None),
            P("chan", "space"),
            P("chan", None, "space", None),
            P(None, "chan"),
        ),
        check_vma=False,
    )
```

```python
import math

import jax
import jax.numpy as jnp
from jax import lax
from jax.experimental import pallas as pl
from jax.experimental.pallas import tpu as pltpu
from jax.sharding import PartitionSpec as P

F32, BF16 = jnp.float32, jnp.bfloat16
HINTS = dict(
    inner=0.1, outer=0.1, back=0.1, out=0.1, sums=0.1, out_sums=0.1, taps=0.1, late_taps=0.1, input=20, pack=0.1, last=0.1, relayout=1.5
)
RATE = 10**9
IN_VMEM = pl.BlockSpec(memory_space=pltpu.VMEM)
ANYWHERE = pl.BlockSpec(memory_space=pl.ANY)


class Place:
    def __init__(self, count):
        self.mids = 2
        self.his = count // 4
        index = lax.axis_index("chan")
        self.core = index % 2
        self.mid = index // 2 % self.mids
        self.hi = index // 2 // self.mids

    def block(self, hi_back, mid_back, core_flip):
        hi = (self.hi + self.his - hi_back) % self.his
        mid = (self.mid + self.mids - mid_back) % self.mids
        core = 1 - self.core if core_flip else self.core
        return hi, mid, core

    def flat(self, hi, mid, core):
        return (hi * self.mids + mid) * 2 + core


def size_of(shape, dtype):
    return math.prod(shape) * jnp.dtype(dtype).itemsize


def rims(near, far):
    odd = lax.axis_index("space") % 2 == 1

    def up(p):
        return jnp.where(odd, near[p].astype(F32), far[p].astype(F32))

    def down(p):
        return jnp.where(odd, far[p].astype(F32), near[p].astype(F32))

    return up, down


def kernel_call(kernel, outs, args, scratch=(), after=(), micros=0.1, places=None):
    used = len(args)

    def run(*refs):
        kernel(*refs[:used], *refs[used + len(after) :])

    held = [x for x in (*args, *outs, *scratch) if jnp.issubdtype(x.dtype, jnp.floating)]
    room = sum(size_of(x.shape, x.dtype) for x in held)
    return pl.pallas_call(
        run,
        out_shape=outs,
        in_specs=[IN_VMEM] * used + [ANYWHERE] * len(after),
        out_specs=places or [IN_VMEM] * len(outs),
        scratch_shapes=list(scratch),
        compiler_params=pltpu.CompilerParams(vmem_limit_bytes=room + 4 * 2**20),
        cost_estimate=pl.CostEstimate(flops=int(micros * RATE), bytes_accessed=0, transcendentals=0),
    )(*args, *after)


def shaped(shape, dtype=BF16):
    return jax.ShapeDtypeStruct(shape, dtype)


def line_home(line, rows):
    plane, row = divmod(line, rows)
    quarter = rows // 4
    core = row // (2 * quarter)
    outer = (row // quarter) in (0, 3)
    return core, outer, plane * quarter + row % quarter


def raw_to_cells(raw, chans, store):
    lines = raw.shape[0] // chans

    @pl.loop(0, chans // 16)
    def _(g):
        group = pl.ds(pl.multiple_of(g * 16, 16), 16)
        for first in range(0, lines, 16):
            block = [raw[pl.ds(pl.multiple_of((g * 16 + c) * lines + first, 16), 16), :] for c in range(16)]
            turned = jnp.swapaxes(jnp.stack([b.astype(F32) for b in block]), 0, 1).astype(BF16)
            for i in range(16):
                store(first + i, group, turned[i])


def write_raw(load, raw, room, sems, chans, lines):
    def copy(start):
        rows = slice(start * lines, (start + 16) * lines)
        return pltpu.make_async_copy(room.at[rows], raw.at[rows], sems.at[start // 16])

    for start in range(0, chans, 16):
        group = slice(start, start + 16)
        for first in range(0, lines, 16):
            block = jnp.stack([load(first + i, group).astype(F32) for i in range(16)])
            turned = jnp.swapaxes(block, 0, 1).astype(BF16)
            for c in range(16):
                at = (start + c) * lines + first
                room[at : at + 16] = turned[c]
        copy(start).start()
    for start in range(0, chans, 16):
        copy(start).wait()


def relayout_images(images, after=()):
    chans, planes, rows, width = images.shape

    def kernel(raw, cells, near, far):
        odd = lax.axis_index("space") % 2 == 1

        def store(line, group, value):
            cells[line, group] = value

        raw_to_cells(raw, chans, store)
        for parity, (first, last) in enumerate(((far, near), (near, far))):

            @pl.when(odd == bool(parity))
            def _():
                @pl.loop(0, planes)
                def _(p):
                    first[p] = cells[p * rows]
                    last[p] = cells[p * rows + rows - 1]

    edge = shaped((planes, chans, width))
    return kernel_call(
        kernel,
        [shaped((planes * rows, chans, width)), edge, edge],
        [images.reshape(-1, width)],
        (),
        after,
        HINTS["relayout"],
    )


def relayout_grad(grad_out, count, after=()):
    chans, planes, rows, width = grad_out.shape
    half = planes * rows // 2

    def kernel(raw, own, other):
        core = Place(count).core
        for mine in range(2):

            @pl.when(core == mine)
            def _():
                def store(line, group, value):
                    home, outer, at = line_home(line, rows)
                    out = own if home == mine else other
                    out[outer * (half // 2) + at, group] = value

                raw_to_cells(raw, chans, store)

    part = shaped((half, chans, width))
    return kernel_call(kernel, [part, part], [grad_out.reshape(-1, width)], (), after, HINTS["relayout"])


def tap_planes(weights, spread, chans, width):
    turned = jnp.concatenate([weights, jnp.zeros((5, chans), F32)], axis=0).T
    for k in range(27):
        spread[k] = jnp.broadcast_to(turned[:, k : k + 1], (chans, width))


def fill_window(padded, line, up, down, planes, rows):
    zero = jnp.zeros(padded.shape[1:], F32)
    for n in range(rows + 2):
        padded[n] = zero
        padded[(planes + 1) * (rows + 2) + n] = zero

    @pl.loop(0, planes)
    def _(p):
        base = (p + 1) * (rows + 2)
        if up is not None:
            padded[base] = up(p)
            padded[base + rows + 1] = down(p)
        for r in range(rows):
            padded[base + 1 + r] = line(p, r).astype(F32)


def depthwise(padded, spread, planes, rows, wanted, store, flipped):
    _, chans, width = padded.shape
    lane = lax.broadcasted_iota(jnp.int32, (8, width), 1)
    deep = 4 // len(wanted)

    def summed(first, group):
        sums = {(d, r): [None] * 3 for d in range(deep) for r in wanted}
        for a in range(3):
            taps = [[spread[26 - 9 * a - 3 * b - e if flipped else 9 * a + 3 * b + e, group] for e in range(3)] for b in range(3)]
            for d in range(deep):
                for line in sorted({r + b for r in wanted for b in range(3)}):
                    cells = padded[(first + d + a) * (rows + 2) + line, group]
                    for b in range(3):
                        if line - b in wanted:
                            held = sums[d, line - b]
                            for e in range(3):
                                term = taps[b][e] * cells
                                held[e] = term if held[e] is None else held[e] + term
        for place, held in sums.items():
            before = jnp.where(lane == 0, 0.0, pltpu.roll(held[0], 1, 1))
            after = jnp.where(lane == width - 1, 0.0, pltpu.roll(held[2], width - 1, 1))
            sums[place] = held[1] + before + after
        return sums

    @pl.loop(0, planes // deep)
    def _(i):
        for start in range(0, chans, 16):
            low = summed(i * deep, slice(start, start + 8))
            high = summed(i * deep, slice(start + 8, start + 16))
            for d, r in low:
                both = jnp.concatenate([low[d, r], high[d, r]], axis=0)
                store(i * deep + d, r, slice(start, start + 16), both)


def hidden_part(cells, near, far, weights, count, planes, rows, outer, after=()):
    _, chans, width = cells.shape
    quarter = rows // 4
    args = [cells, near, far, weights] if outer else [cells, weights]
    wanted = [r for r in range(rows) if ((r // quarter) in (0, 3)) == outer]

    def kernel(*refs):
        cells = refs[0]
        own, other, extra, both = refs[len(args) : len(args) + 4]
        core = Place(count).core
        if outer:
            padded, spread = extra, refs[3]
            up, down = rims(*refs[1:3])
        else:
            padded, spread = refs[-1], extra
            up, down = None, None
            tap_planes(refs[1][...], spread, chans, width)
        fill_window(padded, lambda p, r: cells[p * rows + r], up, down, planes, rows)

        def put(p, r, group, value):
            home, _, at = line_home(r, rows)
            both[home, p * quarter + at, group] = value.astype(BF16)

        depthwise(padded, spread, planes, rows, wanted, put, False)

        @pl.loop(0, planes * quarter)
        def _(i):
            own[i] = both[core, i]
            other[i] = both[1 - core, i]

    part = shaped((planes * quarter, chans, width))
    window = ((planes + 2) * (rows + 2), chans, width)
    outs = [part, part, shaped(window if outer else (27, chans, width), F32)]
    scratch = [pltpu.VMEM((2, planes * quarter, chans, width), BF16)]
    if not outer:
        scratch.append(pltpu.VMEM(window, F32))
    return kernel_call(kernel, outs, args, scratch, after, HINTS["outer" if outer else "inner"])


def picked(table, starts, chans):
    total, wide = table.shape[1], len(starts) * chans
    col = lax.broadcasted_iota(jnp.int32, (total, wide), 1)
    row = lax.broadcasted_iota(jnp.int32, (total, wide), 0)
    want = jnp.zeros((total, wide), jnp.int32)
    for b, start in enumerate(starts):
        want = jnp.where((col >= b * chans) & (col < (b + 1) * chans), start + col - b * chans, want)
    choice = jnp.where(row == want, 1.0, 0.0).astype(BF16)
    return jnp.dot(table, choice, preferred_element_type=F32).astype(BF16)


def pack_grad(own, arrived, filter_own, filter_arrived, count, after=()):
    half, chans, width = own.shape
    part = half // 2
    his, mids = count // 4, 2
    hi_slices, mid_slices = mids * 2 * chans // width, his * 2 * chans // width

    def kernel(own, arrived, filter_own, filter_arrived, *outs):
        place = Place(count)
        table = jnp.concatenate([filter_own[...], filter_arrived[...]], axis=0)
        to_hi, to_mid = outs[: his - 1], outs[his - 1 : his + mids - 2]
        mine_hi, mine_mid = outs[-2:]

        def columns(for_hi, hi, mid):
            if for_hi:
                cells = [(hi, (mid + mids - t) % mids) for t in range(mids)]
            else:
                cells = [((hi + his - s) % his, mid) for s in range(his)]
            starts = [
                place.flat(hi_, mid_, place.core if q == 0 else 1 - place.core) * chans
                for hi_, mid_ in cells
                for q in range(2)
            ]
            return picked(table, starts, chans)

        def put(out, base, value):
            for i in range(value.shape[1] // width):
                out[base + i] = value[:, i * width : (i + 1) * width]

        for refs, offset in ((to_hi, 0), (to_mid, part)):

            @pl.loop(0, part)
            def _(i):
                for ref in refs:
                    ref[i, :chans] = own[offset + i]
                    ref[i, chans:] = arrived[offset + i]

        for s, ref in enumerate(to_hi, 1):
            put(ref, part, columns(True, (place.hi + s) % his, place.mid))
        for t, ref in enumerate(to_mid, 1):
            put(ref, part, columns(False, place.hi, (place.mid + t) % mids))
        put(mine_hi, 0, columns(True, place.hi, place.mid))
        put(mine_mid, 0, columns(False, place.hi, place.mid))

    outs = (
        [shaped((part + hi_slices, 2 * chans, width))] * (his - 1)
        + [shaped((part + mid_slices, 2 * chans, width))] * (mids - 1)
        + [shaped((hi_slices, 2 * chans, width)), shaped((mid_slices, 2 * chans, width))]
    )
    outs = kernel_call(kernel, outs, [own, arrived, filter_own, filter_arrived], (), after, micros=HINTS["pack"])
    return outs[: his - 1], outs[his - 1 : his + mids - 2], outs[-2], outs[-1]


def product_terms(weights, blocks, outs, part, both, width):
    step = math.gcd(part, 4)

    @pl.loop(0, part // step)
    def _(i):
        cells = jnp.concatenate(
            [jnp.concatenate([ref[i * step + j] for ref in blocks], axis=0) for j in range(step)], axis=1
        )
        product = jnp.dot(weights, cells, preferred_element_type=F32)
        for n, out in enumerate(outs):
            for j in range(step):
                term = product[n * both : (n + 1) * both, j * width : (j + 1) * width]
                out[i * step + j] = term.astype(out.dtype)


def back_terms(parts, after=()):
    args, outs, plans = [], [], []
    for mine, arrived, filter_mine, sends in parts:
        slices, both, width = filter_mine.shape
        part = mine.shape[0] - slices
        plans.append((len(args), len(outs), len(arrived), sends, slices, part))
        args += [mine, filter_mine, *arrived]
        outs += [shaped((part, both, width), F32)] + [shaped((part, both, width))] * sends + [shaped(((1 + len(arrived)) * both, slices * width))]
    used = len(args)

    def kernel(*refs):
        for start, out, many, sends, slices, part in plans:
            mine, filter_mine, *arrived = refs[start : start + 2 + many]
            rows = [jnp.concatenate([filter_mine[i] for i in range(slices)], axis=1)]
            for ref in arrived:
                rows.append(jnp.concatenate([ref[part + i] for i in range(slices)], axis=1))
            block = jnp.concatenate(rows, axis=0)
            refs[used + out + sends + 1][...] = block
            turned = block.astype(F32).T.astype(BF16)
            product_terms(turned, [mine, *arrived], refs[used + out : used + out + sends + 1], part, both, width)

    done = kernel_call(kernel, outs, args, (), after, micros=HINTS["back"])
    return [(done[o], done[o + 1 : o + 1 + sends], done[o + 1 + sends]) for _, o, _, sends, _, _ in plans]


def summed_parts(first, second, after=()):
    part, both, width = first[0].shape
    chans = both // 2

    def kernel(*refs):
        outs = refs[-4:]
        for n, terms in enumerate((refs[: len(first)], refs[len(first) : -4])):

            @pl.loop(0, part)
            def _(i):
                total = terms[0][i].astype(F32)
                for term in terms[1:]:
                    total = total + term[i].astype(F32)
                outs[n][i] = total[:chans].astype(BF16)
                outs[2 + n][i] = total[chans:].astype(BF16)

    done = kernel_call(kernel, [shaped((part, chans, width))] * 4, [*first, *second], (), after, HINTS["sums"])
    return done[:2], done[2:]


def edge_rows(own, arrived, count, rows, after=()):
    part, chans, width = own.shape
    quarter = rows // 4
    planes = part // quarter

    def kernel(own, arrived, near, far):
        core = Place(count).core
        odd = lax.axis_index("space") % 2
        for mine in range(2):
            for parity in range(2):

                @pl.when((core == mine) & (odd == parity))
                def _():
                    first, last = (own, arrived) if mine == 0 else (arrived, own)
                    to_first, to_last = (near, far) if parity else (far, near)

                    @pl.loop(0, planes)
                    def _(p):
                        to_first[p] = first[p * quarter]
                        to_last[p] = last[p * quarter + quarter - 1]

    edge = shaped((planes, chans, width))
    return kernel_call(kernel, [edge, edge], [own, arrived], (), after)


def joined(own, arrived, after=()):
    part, chans, width = own[0].shape
    many = len(own)

    def kernel(*refs):
        @pl.loop(0, part)
        def _(i):
            for a, b, out in zip(refs[:many], refs[many : 2 * many], refs[2 * many :]):
                out[i, :chans] = a[i]
                out[i, chans:] = b[i]

    return kernel_call(kernel, [shaped((part, 2 * chans, width))] * many, [*own, *arrived], (), after)


def out_terms(parts, count, after=()):
    args, plans, outs, scratch = [], [], [], []
    for block, hiddens, grads, over_mid in parts:
        part, both, width = hiddens[0].shape
        chans, wide = both // 2, len(hiddens) * both
        plans.append((len(args), len(outs), len(hiddens), len(grads), over_mid))
        args += [block, *hiddens, *grads]
        outs += [shaped((part, both, width), F32), shaped((both, wide), F32)]
        outs += [shaped((part + wide // width, both, width))] * (len(grads) - 1)
        scratch += [pltpu.VMEM((wide, part * width), BF16), pltpu.VMEM((len(grads) * both, part * width), BF16)]
    used = len(args)

    def kernel(*refs):
        place = Place(count)
        rooms = refs[used + len(outs) :]
        for n, (start, out, cols_of, rows_of, over_mid) in enumerate(plans):
            block, hidden = refs[start], refs[start + 1 : start + 1 + cols_of]
            grad = refs[start + 1 + cols_of : start + 1 + cols_of + rows_of]
            keep, gradient, *sends = refs[used + out : used + out + rows_of + 1]
            ordered, lined = rooms[2 * n], rooms[2 * n + 1]
            product_terms(block[...], hidden, [keep, *sends], part, both, width)
            for j in range(part):
                span = slice(j * width, (j + 1) * width)
                for i, ref in enumerate(hidden):
                    hi, mid, _ = place.block(0, i, 0) if over_mid else place.block(i, 0, 0)
                    for q in range(2):
                        core = 1 - place.core if q else place.core
                        at = pl.multiple_of(((mid if over_mid else hi) * 2 + core) * chans, chans)
                        ordered[pl.ds(at, chans), span] = ref[j, q * chans : (q + 1) * chans]
                for i, ref in enumerate(grad):
                    lined[i * both : (i + 1) * both, span] = ref[j]
            pairs = lax.dot_general(lined[...], ordered[...], (((1,), (1,)), ((), ())), preferred_element_type=F32)
            gradient[...] = pairs[:both]
            slices = pairs.shape[1] // width
            for i, send in enumerate(sends, 1):
                value = pairs[i * both : (i + 1) * both].astype(BF16)
                for t in range(slices):
                    send[part + t] = value[:, t * width : (t + 1) * width]

    done = kernel_call(kernel, outs, args, scratch, after, HINTS["out"])
    return [
        (done[out], done[out + 1], done[out + 2 : out + 1 + rows_of]) for _, out, _, rows_of, _ in plans
    ]


def out_sums(first, second, filter_first, filter_second, count, after=()):
    part, both, width = first[0].shape
    chans, his, mids = both // 2, len(first), len(second)
    pair = filter_first.shape[1] // mids

    def kernel(*refs):
        terms = (refs[:his], refs[his : his + mids])
        own_rows, outs = refs[his + mids : his + mids + 2], refs[his + mids + 2 :]
        for n in range(2):

            @pl.loop(0, part)
            def _(i):
                total = terms[n][0][i].astype(F32)
                for term in terms[n][1:]:
                    total = total + term[i].astype(F32)
                outs[n][i] = total[:chans].astype(BF16)
                outs[2 + n][i] = total[chans:].astype(BF16)

        place = Place(count)

        def piece(n, back, columns):
            if back == 0:
                return own_rows[n][:, columns]
            slices = own_rows[n].shape[1] // width
            value = [terms[n][back][part + t].astype(F32) for t in range(slices)]
            return jnp.concatenate(value, axis=1)[:, columns]

        def chosen(n, at, mine, columns):
            value = piece(n, 0, columns)
            for back in range(1, len(terms[n])):
                value = jnp.where((mine + back) % len(terms[n]) == at, piece(n, back, columns), value)
            return value

        for hi in range(his):
            for mid in range(mids):
                block = chosen(0, hi, place.hi, slice(mid * pair, (mid + 1) * pair))
                block = block + chosen(1, mid, place.mid, slice(hi * pair, (hi + 1) * pair))
                at = (hi * mids + mid) * chans
                outs[4][at : at + chans] = block[:chans]
                outs[5][at : at + chans] = block[chans:]

    outs = [shaped((part, chans, width))] * 4 + [shaped((his * mids * chans, pair), F32)] * 2
    args = [*first, *second, filter_first, filter_second]
    done = kernel_call(kernel, outs, args, (), after, HINTS["out_sums"])
    return done[:2], done[2:4], done[4], done[5]


def slab_pieces(own, arrived, taps, slabs, after=()):
    rows = own.shape[0] // slabs
    wide = own.shape[1]

    def kernel(own, arrived, taps, *outs):
        slab = lax.axis_index("space")
        for apart, out in enumerate(outs):
            at = pl.ds(pl.multiple_of(jnp.bitwise_xor(slab, apart) * rows, rows), rows)
            out[:rows] = own[at] + arrived[at]
            out[rows:] = taps[...]

    piece = shaped((rows + taps.shape[0], wide), F32)
    return kernel_call(kernel, [piece] * slabs, [own, arrived, taps], (), after)


def last_outputs(own, arrived, pieces, count, planes, rows, scale, after=()):
    _, chans, width = own[0].shape
    lines, many = planes * rows, len(pieces)

    def kernel(*refs):
        raw, filter_out, tap_out, room, sems = refs[4 + many :]
        core = Place(count).core
        total = refs[4][...]
        for ref in refs[5 : 4 + many]:
            total = total + ref[...]
        total = total * scale
        filter_out[...] = total[:chans]
        tap_out[...] = total[chans : chans + 27, :chans]
        for mine in range(2):

            @pl.when(core == mine)
            def _():
                def load(line, group):
                    home, outer, at = line_home(line, rows)
                    return refs[outer if home == mine else 2 + outer][at, group]

                write_raw(load, raw, room, sems, chans, lines)

    outs = [
        shaped((chans * lines, width)),
        shaped((chans, pieces[0].shape[1]), F32),
        shaped((27, chans), F32),
    ]
    scratch = [pltpu.VMEM((chans * lines, width), BF16), pltpu.SemaphoreType.DMA((chans // 16,))]
    raw, filter_out, tap_out = kernel_call(
        kernel, outs, [*own, *arrived, *pieces], scratch, after, HINTS["last"], [ANYWHERE, IN_VMEM, IN_VMEM]
    )
    return raw.reshape(chans, planes, rows, width), filter_out, tap_out


def input_gradient(inner, outer, near, far, spread, count, planes, rows, after=()):
    _, _, chans, width = inner.shape
    half, lines = rows // 2, planes * rows

    def kernel(own, arrived, near, far, spread, raw, token, padded, cells, room, sems):
        core = Place(count).core
        token[...] = jnp.zeros(token.shape, F32)

        def line(p, r):
            home, at = r // half, r % half
            return jnp.where(core == home, own[at, p], arrived[at, p])

        fill_window(padded, line, *rims(near, far), planes, rows)

        def store(p, r, group, value):
            cells[p * rows + r, group] = value.astype(BF16)

        depthwise(padded, spread, planes, rows, list(range(rows)), store, True)
        write_raw(lambda line, group: cells[line, group], raw, room, sems, chans, lines)

    raw, token = kernel_call(
        kernel,
        [shaped((chans * lines, width)), shaped((8, width), F32)],
        [inner, outer, near, far, spread],
        [
            pltpu.VMEM(((planes + 2) * (rows + 2), chans, width), F32),
            pltpu.VMEM((lines, chans, width), BF16),
            pltpu.VMEM((chans * lines, width), BF16),
            pltpu.SemaphoreType.DMA((chans // 16,)),
        ],
        after,
        HINTS["input"],
        [ANYWHERE, IN_VMEM],
    )
    return raw.reshape(chans, planes, rows, width), token


def tap_sums(padded, back, before, count, planes, rows, others, wide, after=()):
    _, chans, width = padded.shape
    half, quarter = rows // 2, rows // 4
    last = before is not None
    args = [padded, *back] + ([before] if last else [])

    def kernel(padded, inner, outside, *refs):
        out, back = refs[-2 - last], refs[-1 - last]
        sums = refs[-1] if last else out
        core = Place(count).core
        home = 1 - core if others else core
        sums[...] = refs[0][...] if last else jnp.zeros(sums.shape, F32)
        lane = lax.broadcasted_iota(jnp.int32, (8, width), 1)
        deep = max(1, 4 // half)

        @pl.loop(0, planes)
        def _(p):
            for r in range(quarter):
                i = p * quarter + r
                back[r, p] = jnp.where(home == 0, outside[i].astype(F32), inner[i].astype(F32))
                back[quarter + r, p] = jnp.where(home == 0, inner[i].astype(F32), outside[i].astype(F32))

        @pl.loop(0, planes // deep)
        def _(i):
            for start in range(0, chans, 8):
                group = slice(start, start + 8)
                moved = {}
                for d in range(deep):
                    for r in range(half):
                        here = back[r, i * deep + d, group]
                        later = jnp.where(lane == width - 1, 0.0, pltpu.roll(here, width - 1, 1))
                        earlier = jnp.where(lane == 0, 0.0, pltpu.roll(here, 1, 1))
                        moved[d, r] = (later, here, earlier)
                for a in range(3):
                    images = {}
                    for d in range(deep):
                        base = (i * deep + d + a) * (rows + 2) + home * half
                        for line in range(half + 2):
                            images[d, line] = padded[base + line, group]
                    for b in range(3):
                        for e in range(3):
                            term = None
                            for (d, r), values in moved.items():
                                product = images[d, r + b] * values[e]
                                term = product if term is None else term + product
                            sums[9 * a + 3 * b + e, group] += term

        if last:
            row = lax.broadcasted_iota(jnp.int32, (chans, wide), 0)
            col = lax.broadcasted_iota(jnp.int32, (chans, wide), 1)
            for tap in range(27):
                total = jnp.sum(sums[tap], axis=1, keepdims=True)
                out[tap : tap + 1] = jnp.sum(jnp.where(row == col, total, 0.0), axis=0, keepdims=True)
            out[27:] = jnp.zeros((5, wide), F32)

    running = (27, chans, width)
    scratch = [pltpu.VMEM(running, F32)] if last else []
    outs = [shaped((32, wide) if last else running, F32), shaped((half, planes, chans, width), F32)]
    return kernel_call(kernel, outs, args, scratch, after, HINTS["late_taps" if last else "taps"])


def body(images, depth_filter, point_filter, grad_out):
    chans, planes, rows, width = images.shape
    count, slabs = lax.axis_size("chan"), lax.axis_size("space")
    his, mids = count // 4, 2
    place = Place(count)
    grad_scale = 1.0 / math.sqrt(planes * rows * width * slabs)

    def moved(value, target):
        pairs = []
        for i in range(count):
            hi, mid, core = target(i // 2 // mids, i // 2 % mids, i % 2)
            pairs.append((i, (hi % his * mids + mid % mids) * 2 + core))
        return lax.ppermute(value, "chan", pairs)

    def to_core(value):
        return moved(value, lambda hi, mid, core: (hi, mid, 1 - core))

    def along_hi(value, by):
        return moved(value, lambda hi, mid, core: (hi + by, mid, core))

    def along_mid(value, by):
        return moved(value, lambda hi, mid, core: (hi, mid + by, core))

    def halo(near, far):
        swaps = [[(i + d, i + 1 - d) for i in range(first, slabs - 1, 2) for d in range(2)] for first in range(2)]
        return lax.ppermute(near, "space", swaps[0]), lax.ppermute(far, "space", swaps[1])

    def exchanged(value, apart):
        return lax.ppermute(value, "space", [(i, i ^ apart) for i in range(slabs)])

    filter_arrived = to_core(point_filter)
    grad_own, grad_other = relayout_grad(grad_out, count, [filter_arrived])
    grad_arrived = to_core(grad_other)
    cells, near, far = relayout_images(images, [grad_own])
    image_rims = halo(near, far)
    to_hi, to_mid, filter_hi, filter_mid = pack_grad(
        grad_own, grad_arrived, point_filter, filter_arrived, count, [cells]
    )
    grads_hi = [along_hi(value, s) for s, value in enumerate(to_hi, 1)]
    grads_mid = [along_mid(value, t) for t, value in enumerate(to_mid, 1)]

    windows = (cells, *image_rims)
    plan = (count, planes, rows)
    inner_own, inner_other, spread = hidden_part(*windows, depth_filter, *plan, False, [to_hi[0]])
    inner_arrived = to_core(inner_other)
    outer_own, outer_other, padded = hidden_part(*windows, spread, *plan, True, [inner_own])
    outer_arrived = to_core(outer_other)
    hidden_first, hidden_second = joined([inner_own, outer_own], [inner_arrived, outer_arrived])
    hiddens_mid = [hidden_first] + [along_mid(hidden_first, t) for t in range(1, mids)]
    hiddens_hi = [hidden_second] + [along_hi(hidden_second, s) for s in range(1, his)]

    (keep_first, send_first, block_first), (keep_second, send_second, block_second) = back_terms(
        [(to_hi[0], grads_hi, filter_hi, mids - 1), (to_mid[0], grads_mid, filter_mid, his - 1)], [hidden_first]
    )
    back_first = [keep_first] + [along_mid(value, -t) for t, value in enumerate(send_first, 1)]
    back_second = [keep_second] + [along_hi(value, -s) for s, value in enumerate(send_second, 1)]

    (out_first, pg_first, send_first), (out_second, pg_second, send_second) = out_terms(
        [
            (block_first, hiddens_mid, [to_hi[0], *grads_hi], True),
            (block_second, hiddens_hi, [to_mid[0], *grads_mid], False),
        ],
        count,
        [keep_first],
    )
    latest = out_first
    out_first = [out_first] + [along_hi(value, -s) for s, value in enumerate(send_first, 1)]
    out_second = [out_second] + [along_mid(value, -t) for t, value in enumerate(send_second, 1)]

    back_own, back_other = summed_parts(back_first, back_second, [latest])
    back_arrived = [to_core(value) for value in back_other]
    wide = his * mids * 2 * chans // slabs
    taps, back_own_lines = tap_sums(padded, back_own, None, *plan, False, wide)
    edges = edge_rows(back_own[1], back_arrived[1], count, rows, [taps])
    back_rims = halo(*edges)
    taps, back_arrived_lines = tap_sums(padded, back_arrived, taps, *plan, True, wide, [edges[0]])
    out_own, out_other, own, other = out_sums(out_first, out_second, pg_first, pg_second, count, [taps])
    out_arrived = [to_core(value) for value in out_other]
    chip_arrived = to_core(other)
    if own.shape[1] != wide:

        def by_slab(value):
            value = value.reshape(his * mids, chans, -1).swapaxes(0, 1).reshape(chans, slabs, wide)
            return value.swapaxes(0, 1).reshape(-1, wide)

        own, chip_arrived = by_slab(own), by_slab(chip_arrived)
    pieces = slab_pieces(own, chip_arrived, taps, slabs)
    input_grad, latest = input_gradient(back_own_lines, back_arrived_lines, *back_rims, spread, *plan, [pieces[0]])
    pieces = [pieces[0]] + [exchanged(piece, apart) for apart, piece in enumerate(pieces[1:], 1)]
    block_out, point_grad, depth_grad = last_outputs(out_own, out_arrived, pieces, *plan, grad_scale, [latest])
    return block_out, point_grad, input_grad, depth_grad


def solution(mesh):
    placed = (
        P("chan", None, "space", None),
        P(None, "chan"),
        P("chan", None),
        P("chan", None, "space", None),
    )
    return jax.shard_map(
        body,
        mesh=mesh,
        in_specs=placed,
        out_specs=(
            P("chan", None, "space", None),
            P("chan", "space"),
            P("chan", None, "space", None),
            P(None, "chan"),
        ),
        check_vma=False,
    )
```
